512 devices in a mesh: shard: 32 (over z, x), group: 16 (over y, core).
Axes of the slice: x: 4, y: 8, z: 8, core: 2. Of those that a mesh axis runs over, the one named last changes fastest.
Arguments:
- embeddings: bfloat16 [262144, 1024], P(('shard', 'group')), may hold values from -0.1875 to 0.1875
- cluster_key: int32 [262144, 1], P(('shard', 'group')), may hold values from 0 to 511; in each aligned block of 512 rows (0 to 511, 512 to 1023, ...) at most 2 rows name the same one
- child_first: int32 [262144], P(('shard', 'group')), may hold values from 0 to 511
- child_second: int32 [262144], P(('shard', 'group')), may hold values from 0 to 511
- coarse_centroids: bfloat16 [32, 512, 1024], P('shard'), may hold values from -0.1875 to 0.1875
- fine_centroids: bfloat16 [16, 512, 1024], P('group'), may hold values from -0.1875 to 0.1875
Outputs:
- coarse_new: bfloat16 [32, 512, 1024], P('shard')
- fine_new: bfloat16 [16, 512, 1024], P('group')
- coarse_cost: float32 [32, 512], P('shard')
- fine_cost: float32 [16, 512], P('group')
The draws below stay inside these ranges and needn't reach their ends.
Inputs may be any that keep to these rules, and one draw needn't show every extreme that they name: `cluster_key`: in every aligned block of 512 documents (the documents of one device) no key appears more than 2 times.
All inputs are finite; a program needn't handle non-finite values.
Results may differ from the reference program's by a relative error of at most 0.022.
Values may be sent and summed in bfloat16 or wider, within the bound.
No kernel may reach another device: no remote copies, remote signals or barrier semaphores. Data moves between devices by JAX's collectives and lax.ppermute only.
A program may use at most 128 MiB of HBM per device.

```python
import math
import jax
import jax.numpy as jnp
import numpy as np
from jax import lax

D = 1024
K = 512
ROWS_DEV = 512
ROWS = 262144
SLOTS = 2
N_SHARD = 32
N_GROUP = 16


def with_ends(drawn, own_key, smallest, top_value):
    dims = drawn.shape
    place = [jax.random.randint(jax.random.fold_in(own_key, axis), (), 0, dims[axis]) for axis in range(len(dims))]
    drawn = drawn.at[tuple(place)].set(smallest)
    longest = dims.index(max(dims))
    place[longest] = (place[longest] + 1) % dims[longest]
    return drawn.at[tuple(place)].set(top_value)


def levels(rng, shape, cuts, least, top_value):
    gain = 1.0
    for dim, blocks in cuts:
        draws = jax.random.uniform(jax.random.fold_in(jax.random.fold_in(rng, 6), dim), (blocks,), jnp.float32, least / len(cuts), top_value / len(cuts))
        gain = gain * jnp.repeat(jnp.exp(draws), shape[dim] // blocks).reshape((-1,) + (1,) * (len(shape) - 1 - dim))
    return gain


def assign_block(rng, own, number, rows, number_of, top, bound, slope):
    ranking = jax.random.permutation(rng, number_of)
    crowded, ordinary = load_shares(number_of, rows * top, bound, slope, True), load_shares(number_of, rows * top, bound, slope, False)
    places = jnp.arange(number_of)

    def named(sizes, offset_by):
        used = int((sizes > 0).sum())
        fixed = max(1, used // 4)
        passed = fixed + (places - fixed + offset_by * (used - fixed)) % max(1, number_of - fixed)
        return jnp.zeros((number_of,), jnp.int32).at[ranking[jnp.where(places < fixed, places, passed)]].set(jnp.asarray(sizes, jnp.int32))

    sizes = jnp.where(number % 4 == 0, named(crowded, number // 4), named(ordinary, number - number // 4 - 1))
    mixed = jax.random.permutation(jax.random.fold_in(own, 3), number_of)
    giver, receiver = mixed[0:number_of // 2 * 2:2], mixed[1:number_of // 2 * 2:2]
    room = jnp.minimum(sizes[giver] - 1, bound - sizes[receiver]) // 2
    room = jnp.where((giver == ranking[0]) | (receiver == ranking[0]) | (sizes[receiver] == 0), 0, jnp.maximum(room, 0))
    passed = jax.random.randint(jax.random.fold_in(own, 4), (number_of // 2,), 0, 1 << 20) % (room + 1)
    sizes = sizes.at[giver].add(-passed).at[receiver].add(passed)
    members = jnp.searchsorted(jnp.cumsum(sizes), jnp.arange(rows * top), side="right").astype(jnp.int32)
    grid = members.reshape(top, rows).T
    grid = grid[jax.random.permutation(jax.random.fold_in(own, 1), rows)]
    offset_by = jax.random.randint(jax.random.fold_in(own, 2), (rows, 1), 0, top)
    return jnp.take_along_axis(grid, (jnp.arange(top)[None, :] + offset_by) % top, axis=1)


def load_shares(amount, total, limit, skew, full):
    loads = [(1 << 20) // math.isqrt(grade ** skew) + 1 for grade in range(1, amount + 1)]
    largest = limit if full else min(limit, max(-(-total // amount), total * loads[0] // sum(loads)))
    least = 1 if total - largest >= amount - 1 else 0
    given, surplus = [largest] + [least] * (amount - 1), total - largest - least * (amount - 1)
    while surplus > 0:
        free = [i for i in range(1, amount) if given[i] < largest] or [i for i in range(1, amount) if given[i] < limit]
        pool, budget = sum([loads[i] for i in free]), surplus
        for i in free:
            more = min(limit - given[i], max(1, budget * loads[i] // pool), surplus)
            given[i] = given[i] + more
            surplus = surplus - more
    return np.array(given)


def gaussian(stream_key, shape, width, most, cuts=(), held_as=jnp.bfloat16):
    gain = levels(stream_key, shape, cuts, -0.22, 0.18) if cuts else 1.0
    entries = jax.random.normal(stream_key, shape, jnp.float32) * width * gain
    return jnp.minimum(jnp.maximum(entries, -most), most).astype(held_as)


def setup_inputs(seed: int = 0) -> dict:
    splits = jax.random.split(jax.random.key(seed), 7)
    embeddings = gaussian(splits[0], (ROWS, D), 0.03125, 0.1875, ((0, 512),))
    cluster_key_keys = jax.random.split(jax.random.fold_in(splits[1], 1), ROWS // ROWS_DEV)
    cluster_key_turns = jax.random.permutation(jax.random.fold_in(splits[1], 3), ROWS // ROWS_DEV)
    cluster_key = jax.vmap(lambda own, number: assign_block(jax.random.fold_in(splits[1], 2), own, number, ROWS_DEV, N_SHARD * N_GROUP, 1, SLOTS, 2))(cluster_key_keys, cluster_key_turns).reshape((ROWS, 1))
    child_first = with_ends(jax.random.randint(splits[2], (ROWS,), 0, K), jax.random.fold_in(splits[2], 1), 0, K - 1).astype(jnp.int32)
    child_second = with_ends(jax.random.randint(splits[3], (ROWS,), 0, K), jax.random.fold_in(splits[3], 1), 0, K - 1).astype(jnp.int32)
    coarse_centroids = gaussian(splits[4], (N_SHARD, K, D), 0.03125, 0.1875, ((0, 32),))
    fine_centroids = gaussian(splits[5], (N_GROUP, K, D), 0.03125, 0.1875, ((0, 16),))
    return dict(embeddings=embeddings, cluster_key=cluster_key, child_first=child_first, child_second=child_second, coarse_centroids=coarse_centroids, fine_centroids=fine_centroids)


def margins_of(rows, assign, cents):
    products = jnp.dot(rows, cents.T, preferred_element_type=jnp.float32)
    cent_f = cents.astype(jnp.float32)
    squares = jnp.sum(cent_f * cent_f, axis=1)
    scores = squares[None, :] - 2.0 * products
    picked = jnp.take_along_axis(scores, assign[:, None], axis=1)[:, 0]
    return picked - jnp.min(scores, axis=1)


def rounded(value):
    return lax.optimization_barrier(value.astype(jnp.bfloat16)).astype(jnp.float32)


def reference(embeddings, cluster_key, child_first, child_second, coarse_centroids, fine_centroids):
    keys = cluster_key[:, 0]
    first = keys // N_GROUP
    source_group = (jnp.arange(ROWS, dtype=jnp.int32) // ROWS_DEV) % N_GROUP
    limit_one = min(ROWS, N_SHARD * N_GROUP * N_GROUP * SLOTS)

    def coarse_one(s):
        chosen = first == s
        index = jnp.nonzero(chosen, size=limit_one, fill_value=0)[0].astype(jnp.int32)
        live = jnp.arange(limit_one, dtype=jnp.int32) < jnp.sum(chosen.astype(jnp.int32))
        rows = embeddings[index]
        assign = child_first[index]
        margin = jnp.where(live, margins_of(rows, assign, coarse_centroids[s]), 0.0)
        segment = jnp.where(live, source_group[index] * K + assign, N_GROUP * K)
        sums = jax.ops.segment_sum(rows.astype(jnp.float32), segment, N_GROUP * K)
        counts = jax.ops.segment_sum(live.astype(jnp.float32), segment, N_GROUP * K)
        costs = jax.ops.segment_sum(margin, segment, N_GROUP * K)
        sums = jnp.sum(rounded(sums).reshape(N_GROUP, K, D), axis=0)
        counts = jnp.sum(rounded(counts).reshape(N_GROUP, K), axis=0)
        costs = jnp.sum(rounded(costs).reshape(N_GROUP, K), axis=0)
        return sums, counts, costs

    coarse_sum, coarse_count, coarse_cost = lax.map(coarse_one, jnp.arange(N_SHARD, dtype=jnp.int32))
    coarse_f = (coarse_sum + coarse_centroids.astype(jnp.float32)) / (coarse_count[:, :, None] + 1.0)
    limit_two = min(ROWS, N_SHARD * N_GROUP * SLOTS)

    def fine_step(pair, carry):
        sums_all, counts_all, costs_all = carry
        s = pair // N_GROUP
        g = pair % N_GROUP
        chosen = keys == pair
        index = jnp.nonzero(chosen, size=limit_two, fill_value=0)[0].astype(jnp.int32)
        live = jnp.arange(limit_two, dtype=jnp.int32) < jnp.sum(chosen.astype(jnp.int32))
        centers = coarse_f[s][child_first[index]]
        residual = (embeddings[index].astype(jnp.float32) - centers).astype(jnp.bfloat16)
        assign = child_second[index]
        margin = jnp.where(live, margins_of(residual, assign, fine_centroids[g]), 0.0)
        segment = jnp.where(live, assign, K)
        sums = rounded(jax.ops.segment_sum(residual.astype(jnp.float32), segment, K))
        counts = rounded(jax.ops.segment_sum(live.astype(jnp.float32), segment, K))
        costs = rounded(jax.ops.segment_sum(margin, segment, K))
        return (sums_all.at[g].add(sums), counts_all.at[g].add(counts), costs_all.at[g].add(costs))

    start = (jnp.zeros((N_GROUP, K, D), jnp.float32), jnp.zeros((N_GROUP, K), jnp.float32), jnp.zeros((N_GROUP, K), jnp.float32))
    fine_sum, fine_count, fine_cost = lax.fori_loop(0, N_SHARD * N_GROUP, fine_step, start)
    fine_f = (fine_sum + fine_centroids.astype(jnp.float32)) / (fine_count[:, :, None] + 1.0)
    return coarse_f.astype(jnp.bfloat16), fine_f.astype(jnp.bfloat16), coarse_cost, fine_cost
```

```python
import jax
import jax.numpy as jnp
from jax import lax
from jax.sharding import Mesh
from jax.sharding import PartitionSpec as P

SHARD = ("z", "x")
GROUP = ("y", "core")
ALL = SHARD + GROUP
SLOTS = 2
EXTRA = 128


def exchange(blocks, axes):
    return lax.all_to_all(blocks, axes, split_axis=0, concat_axis=0, tiled=True)


def columns(values, rows):
    lanes = lax.broadcasted_iota(jnp.int32, (rows, EXTRA), 1)
    out = jnp.zeros((rows, EXTRA), jnp.bfloat16)
    for lane, value in enumerate(values):
        out = jnp.where(lanes == lane, value.astype(jnp.bfloat16)[:, None], out)
    return out


def halves(value):
    high = value.astype(jnp.bfloat16)
    return high, (value - high.astype(jnp.float32)).astype(jnp.bfloat16)


def level_sums(rows, member, live, centroids):
    products = lax.dot_general(
        rows, centroids, (((1,), (1,)), ((), ())), preferred_element_type=jnp.float32
    )
    cent_f = centroids.astype(jnp.float32)
    squares = jnp.sum(cent_f * cent_f, axis=1)
    scores = squares[None, :] - 2.0 * products
    assigned = jnp.sum(jnp.where(member, scores, 0.0), axis=1)
    margin = jnp.where(live, assigned - jnp.min(scores, axis=1), 0.0)
    extra = columns((live,) + halves(margin), rows.shape[0])
    return lax.dot_general(
        member.astype(jnp.bfloat16),
        jnp.concatenate([rows, extra], axis=1),
        (((0,), (0,)), ((), ())),
        preferred_element_type=jnp.float32,
    ).astype(jnp.bfloat16)


def merged(partial, axes, parts, mine, centroids):
    children, wide = partial.shape
    each = children // parts
    width = wide - EXTRA
    arrived = exchange(partial.reshape(parts, each, wide), axes)
    total = jnp.sum(arrived.astype(jnp.float32), axis=0)
    old = lax.dynamic_slice_in_dim(centroids, mine * each, each, 0).astype(jnp.float32)
    fresh = (total[:, :width] + old) / (total[:, width : width + 1] + 1.0)
    cost = total[:, width + 1] + total[:, width + 2]
    return jnp.concatenate([fresh.astype(jnp.bfloat16), columns(halves(cost), each)], axis=1)


def spread(block, axes, parts):
    return exchange(jnp.broadcast_to(block[None], (parts,) + block.shape), axes)


def cost_of(full, width):
    tail = full[:, width : width + 2].astype(jnp.float32)
    return tail[:, 0] + tail[:, 1]


def local(embeddings, cluster_key, child_first, child_second, coarse_centroids, fine_centroids):
    n_shard = lax.axis_size(SHARD)
    n_group = lax.axis_size(GROUP)
    rows_dev, width = embeddings.shape
    children = coarse_centroids.shape[1]
    devices = n_shard * n_group
    slots = devices * SLOTS
    coarse, fine = coarse_centroids[0], fine_centroids[0]

    keys = cluster_key[:, 0]
    rows_i = lax.broadcasted_iota(jnp.int32, (rows_dev, rows_dev), 0)
    cols_i = lax.broadcasted_iota(jnp.int32, (rows_dev, rows_dev), 1)
    same = (keys[:, None] == keys[None, :]) & (rows_i < cols_i)
    place = keys * SLOTS + jnp.sum(same.astype(jnp.int32), axis=0)
    move = lax.broadcasted_iota(jnp.int32, (slots, rows_dev), 0) == place[None, :]
    codes = columns(
        (
            jnp.ones((rows_dev,), jnp.int32),
            child_first // 16,
            child_first % 16,
            child_second // 16,
            child_second % 16,
        ),
        rows_dev,
    )
    layout = lax.dot_general(
        move.astype(jnp.bfloat16),
        jnp.concatenate([embeddings, codes], axis=1),
        (((1,), (0,)), ((), ())),
        preferred_element_type=jnp.float32,
    ).astype(jnp.bfloat16)
    arrived = exchange(layout.reshape(devices, SLOTS, width + EXTRA), ALL)
    arrived = arrived.reshape(slots, width + EXTRA)
    rows = arrived[:, :width]
    tail = arrived[:, width : width + 5].astype(jnp.int32)
    live = tail[:, 0] > 0
    labels = lax.broadcasted_iota(jnp.int32, (slots, children), 1)
    member_one = ((tail[:, 1] * 16 + tail[:, 2])[:, None] == labels) & live[:, None]
    member_two = ((tail[:, 3] * 16 + tail[:, 4])[:, None] == labels) & live[:, None]

    partial_one = level_sums(rows, member_one, live, coarse)
    block_one = merged(partial_one, GROUP, n_group, lax.axis_index(GROUP), coarse)
    n_y = lax.axis_size("y")
    own = spread(block_one, "y", n_y)
    other = lax.ppermute(own, "core", [(0, 1), (1, 0)])
    even = lax.axis_index("core") == 0
    full_one = jnp.stack(
        [jnp.where(even, own, other), jnp.where(even, other, own)], axis=1
    ).reshape(children, width + EXTRA)
    coarse_new = full_one[:, :width]

    center = lax.dot_general(
        member_one.astype(jnp.bfloat16),
        coarse_new,
        (((1,), (0,)), ((), ())),
        preferred_element_type=jnp.float32,
    )
    residual = (rows.astype(jnp.float32) - center).astype(jnp.bfloat16)
    partial_two = level_sums(residual, member_two, live, fine)
    block_two = merged(partial_two, SHARD, n_shard, lax.axis_index(SHARD), fine)
    full_two = spread(block_two, SHARD, n_shard).reshape(children, width + EXTRA)
    return (
        coarse_new[None],
        full_two[:, :width][None],
        cost_of(full_one, width)[None],
        cost_of(full_two, width)[None],
    )


def solution(mesh):
    torus = Mesh(mesh.devices.reshape(-1, 4, mesh.shape["group"] // 2, 2), ALL)
    placed = (
        P(ALL, None),
        P(ALL, None),
        P(ALL),
        P(ALL),
        P(SHARD, None, None),
        P(GROUP, None, None),
    )
    return jax.shard_map(
        local,
        mesh=torus,
        in_specs=placed,
        out_specs=(
            P(SHARD, None, None),
            P(GROUP, None, None),
            P(SHARD, None),
            P(GROUP, None),
        ),
        check_vma=False,
    )
```

```python
import functools

import jax
import jax.numpy as jnp
from jax import lax
from jax.experimental import pallas as pl
from jax.experimental.pallas import tpu as pltpu
from jax.sharding import Mesh
from jax.sharding import PartitionSpec as P

SHARD = ("z", "x")
GROUP = ("y", "core")
ALL = SHARD + GROUP
SLOTS = 2
LANES = 128
EXTRA = 16
DIGIT = 16
F32 = jnp.float32
BF16 = jnp.bfloat16


def exchange(blocks, axes):
    return lax.all_to_all(blocks, axes, split_axis=0, concat_axis=0, tiled=True)


def iota(shape, dim):
    return lax.broadcasted_iota(jnp.int32, shape, dim)


def matmul(a, b, dims):
    return lax.dot_general(a, b, (dims, ((), ())), preferred_element_type=F32)


def kernel_call(body, name, flops, moved, **rest):
    return pl.pallas_call(
        body,
        name=name,
        cost_estimate=pl.CostEstimate(flops=flops, bytes_accessed=moved, transcendentals=0),
        compiler_params=pltpu.CompilerParams(vmem_limit_bytes=48 * 2**20),
        **rest,
    )


def whole(shape):
    return pl.BlockSpec(shape, lambda *_: (0,) * len(shape))


def place_body(info_ref, emb_ref, out_ref, wide_ref, place_ref):
    count, width = emb_ref.shape
    devices, slots, wide = out_ref.shape
    step = pl.program_id(0)

    @pl.when(step == 0)
    def _():
        info = info_ref[...]
        turned = jnp.transpose(info.astype(F32)).astype(jnp.int32)
        keys_row, keys_col = info[0:1, :], turned[:, 0:1]
        earlier = (keys_col == keys_row) & (iota((count, count), 0) < iota((count, count), 1))
        rank = jnp.sum(earlier.astype(jnp.int32), axis=0, keepdims=True)
        place_ref[...] = jnp.broadcast_to(keys_row * slots + rank, place_ref.shape)
        one, two = turned[:, 1:2], turned[:, 2:3]
        lane = iota((count, LANES), 1)
        codes = jnp.where(lane == 0, 1, 0)
        for index, value in enumerate((one // DIGIT, one % DIGIT, two // DIGIT, two % DIGIT)):
            codes = jnp.where(lane == index + 1, value, codes)
        wide_ref[:, :width] = emb_ref[...]
        wide_ref[:, width:] = codes.astype(F32).astype(BF16)

    block = devices * slots
    target = iota((block, count), 0) + step * block
    move = (target == place_ref[0:1, :]).astype(F32).astype(BF16)
    moved = matmul(move, wide_ref[...], ((1,), (0,))).astype(BF16)
    out_ref[...] = moved.reshape(devices, slots, wide)


def place(info, embeddings, devices, steps):
    count, width = embeddings.shape
    wide = width + LANES
    each = devices // steps
    return kernel_call(
        place_body,
        "place",
        2 * devices * SLOTS * count * wide,
        2 * (count * width + devices * SLOTS * wide),
        grid=(steps,),
        in_specs=[whole(info.shape), whole(embeddings.shape)],
        out_specs=pl.BlockSpec((each, SLOTS, wide), lambda i: (i, 0, 0)),
        out_shape=jax.ShapeDtypeStruct((devices, SLOTS, wide), BF16),
        scratch_shapes=[pltpu.VMEM((count, wide), BF16), pltpu.VMEM((8, count), jnp.int32)],
    )(info, embeddings)


def label_row(tail, first):
    turned = jnp.transpose(tail.astype(F32))
    label = turned[first : first + 1, :] * DIGIT + turned[first + 1 : first + 2, :]
    return jnp.where(turned[0:1, :] > 0, label, -1.0).astype(jnp.int32)


def label_col(tail, first):
    tail = tail.astype(F32)
    label = tail[:, first : first + 1] * DIGIT + tail[:, first + 1 : first + 2]
    return jnp.where(tail[:, 0:1] > 0, label, -1.0).astype(jnp.int32)


def add_sums(step, rows, label, sums_ref, counts_ref):
    children, count = sums_ref.shape[0], rows.shape[0]
    member = (iota((children, count), 0) == label).astype(F32).astype(BF16)
    sums = matmul(member, rows, ((1,), (0,)))
    counts = matmul(jnp.ones((EXTRA, count), BF16), member, ((1,), (1,)))

    @pl.when(step == 0)
    def _():
        sums_ref[...] = sums
        counts_ref[...] = counts

    @pl.when(step > 0)
    def _():
        sums_ref[...] += sums
        counts_ref[...] += counts


def write_blocks(out_ref, sums_ref, counts_ref):
    parts, tall, _ = out_ref.shape
    children, width = sums_ref.shape
    each = children // parts
    for j in range(width // LANES):
        piece = sums_ref[:, j * LANES : (j + 1) * LANES].astype(BF16)
        out_ref[:, j * each : (j + 1) * each, :] = piece.reshape(parts, each, LANES)
    counts = counts_ref[...].astype(BF16)
    for h in range(parts):
        chunk = h * each // LANES * LANES
        out_ref[h, tall - EXTRA :, :] = counts[:, chunk : chunk + LANES]


def first_body(arrived_ref, rows_ref, out_ref, sums_ref, counts_ref):
    count, wide = rows_ref.shape
    step = pl.program_id(0)
    rows = arrived_ref[...].reshape(count, wide)
    rows_ref[...] = rows
    width = wide - LANES
    add_sums(step, rows[:, :width], label_row(rows[:, width:], 1), sums_ref, counts_ref)

    @pl.when(step == pl.num_programs(0) - 1)
    def _():
        write_blocks(out_ref, sums_ref, counts_ref)


def first_sums(arrived, children, parts, steps):
    devices, slots, wide = arrived.shape
    width = wide - LANES
    total = devices * slots
    tall = children // parts * (width // LANES) + EXTRA
    return kernel_call(
        first_body,
        "first_sums",
        2 * total * children * width,
        4 * total * wide + 2 * children * width,
        grid=(steps,),
        in_specs=[pl.BlockSpec((devices // steps, slots, wide), lambda i: (i, 0, 0))],
        out_specs=[
            pl.BlockSpec((total // steps, wide), lambda i: (i, 0)),
            whole((parts, tall, LANES)),
        ],
        out_shape=[
            jax.ShapeDtypeStruct((total, wide), BF16),
            jax.ShapeDtypeStruct((parts, tall, LANES), BF16),
        ],
        scratch_shapes=[pltpu.VMEM((children, width), F32), pltpu.VMEM((EXTRA, children), F32)],
    )(arrived)


def margin_body(first, rows_ref, tail_ref, cents_ref, squares_ref, out_ref, costs_ref):
    step = pl.program_id(0)
    products = matmul(rows_ref[...], cents_ref[...], ((1,), (1,)))
    scores = squares_ref[...] - 2.0 * products
    member = iota(scores.shape, 1) == label_col(tail_ref[...], first)
    assigned = jnp.sum(jnp.where(member, scores, 0.0), axis=1, keepdims=True)
    margin = assigned - jnp.min(scores, axis=1, keepdims=True)
    costs = jnp.sum(jnp.where(member, margin, 0.0), axis=0, keepdims=True)

    @pl.when(step == 0)
    def _():
        costs_ref[...] = jnp.broadcast_to(costs, costs_ref.shape)

    @pl.when(step > 0)
    def _():
        costs_ref[...] += jnp.broadcast_to(costs, costs_ref.shape)

    @pl.when(step == pl.num_programs(0) - 1)
    def _():
        costs = costs_ref[0:1, :]
        high = costs.astype(BF16).astype(F32)
        chunks = costs.shape[1] // LANES
        index = iota(out_ref.shape, 0)
        out = jnp.zeros(out_ref.shape, F32)
        for q in range(chunks):
            lanes = slice(q * LANES, (q + 1) * LANES)
            out = jnp.where(index == q, high[:, lanes], out)
            out = jnp.where(index == q + chunks, (costs - high)[:, lanes], out)
        out_ref[...] = out.astype(BF16)


def margins(rows, codes, centroids, squares, first, steps):
    total = rows.shape[0]
    children, width = centroids.shape
    tail_at = codes.shape[1] // LANES - 1
    return kernel_call(
        functools.partial(margin_body, first),
        "margins",
        2 * total * children * width,
        2 * (total + children) * width,
        grid=(steps,),
        in_specs=[
            pl.BlockSpec((total // steps, width), lambda i: (i, 0)),
            pl.BlockSpec((total // steps, LANES), lambda i: (i, tail_at)),
            whole(centroids.shape),
            whole(squares.shape),
        ],
        out_specs=whole((EXTRA, LANES)),
        out_shape=jax.ShapeDtypeStruct((EXTRA, LANES), BF16),
        scratch_shapes=[pltpu.VMEM((8, children), F32)],
    )(rows, codes, centroids, squares)


def merge_body(mine_ref, arrived_ref, old_ref, costs_ref, out_ref):
    copies, tall, _ = out_ref.shape
    each, width = old_ref.shape
    total = jnp.sum(arrived_ref[...].astype(F32), axis=0)
    counts = total[tall - EXTRA : tall - EXTRA + 1, :]
    start = lax.rem(mine_ref[0] * each, LANES)
    mask = iota((each, LANES), 1) == iota((each, LANES), 0) + start
    count = jnp.sum(jnp.where(mask, counts, 0.0), axis=1, keepdims=True)
    for j in range(width // LANES):
        old = old_ref[:, j * LANES : (j + 1) * LANES].astype(F32)
        fresh = (total[j * each : (j + 1) * each, :] + old) / (count + 1.0)
        out_ref[:, j * each : (j + 1) * each, :] = jnp.broadcast_to(
            fresh.astype(BF16)[None], (copies, each, LANES)
        )
    out_ref[:, tall - EXTRA :, :] = jnp.broadcast_to(costs_ref[...][None], (copies, EXTRA, LANES))


def merge(mine, arrived, centroids, costs, copies):
    parts, tall, _ = arrived.shape
    children, width = centroids.shape
    each = children // parts
    return kernel_call(
        merge_body,
        "merge",
        arrived.size,
        2 * (arrived.size + each * width + copies * tall * LANES),
        grid_spec=pltpu.PrefetchScalarGridSpec(
            num_scalar_prefetch=1,
            grid=(1,),
            in_specs=[
                pl.BlockSpec(arrived.shape, lambda i, mine: (0, 0, 0)),
                pl.BlockSpec((each, width), lambda i, mine: (mine[0], 0)),
                pl.BlockSpec(costs.shape, lambda i, mine: (0, 0)),
            ],
            out_specs=pl.BlockSpec((copies, tall, LANES), lambda i, mine: (0, 0, 0)),
        ),
        out_shape=jax.ShapeDtypeStruct((copies, tall, LANES), BF16),
    )(mine, arrived, centroids, costs)


def cost_sum(costs, chunks):
    total = jnp.sum(costs.astype(F32), axis=0)
    return total[0:chunks, :] + total[chunks : 2 * chunks, :]


def second_body(
    core_ref, rows_ref, own_ref, other_ref, new_ref, cost_ref, residual_ref, out_ref, sums_ref, counts_ref
):
    step = pl.program_id(0)
    parts, tall, _ = own_ref.shape
    children, width = new_ref.shape
    each = children // (2 * parts)

    @pl.when(step == 0)
    def _():
        core = core_ref[0]
        for ref, side in ((own_ref, core), (other_ref, 1 - core)):
            for y in range(parts):
                at = pl.ds(pl.multiple_of((2 * y + side) * each, each), each)
                for j in range(width // LANES):
                    new_ref[at, j * LANES : (j + 1) * LANES] = ref[y, j * each : (j + 1) * each, :]
        chunks = children // LANES
        cost_ref[...] = cost_sum(own_ref[:, tall - EXTRA :, :], chunks) + cost_sum(
            other_ref[:, tall - EXTRA :, :], chunks
        )

    rows = rows_ref[:, :width]
    tail = rows_ref[:, width:]
    count = rows.shape[0]
    picked = (iota((count, children), 1) == label_col(tail, 1)).astype(F32).astype(BF16)
    center = matmul(picked, new_ref[...], ((1,), (0,)))
    residual = (rows.astype(F32) - center).astype(BF16)
    residual_ref[...] = residual
    add_sums(step, residual, label_row(tail, 3), sums_ref, counts_ref)

    @pl.when(step == pl.num_programs(0) - 1)
    def _():
        write_blocks(out_ref, sums_ref, counts_ref)


def second_sums(core, rows, own, other, children, parts, steps):
    total, wide = rows.shape
    width = wide - LANES
    tall = children // parts * (width // LANES) + EXTRA
    chunks = children // LANES
    fixed = lambda shape: pl.BlockSpec(shape, lambda i, core: (0,) * len(shape))
    return kernel_call(
        second_body,
        "second_sums",
        4 * total * children * width,
        4 * total * wide + 6 * children * width,
        grid_spec=pltpu.PrefetchScalarGridSpec(
            num_scalar_prefetch=1,
            grid=(steps,),
            in_specs=[
                pl.BlockSpec((total // steps, wide), lambda i, core: (i, 0)),
                fixed(own.shape),
                fixed(other.shape),
            ],
            out_specs=[
                fixed((children, width)),
                fixed((chunks, LANES)),
                pl.BlockSpec((total // steps, width), lambda i, core: (i, 0)),
                fixed((parts, tall, LANES)),
            ],
            scratch_shapes=[
                pltpu.VMEM((children, width), F32),
                pltpu.VMEM((EXTRA, children), F32),
            ],
        ),
        out_shape=[
            jax.ShapeDtypeStruct((children, width), BF16),
            jax.ShapeDtypeStruct((chunks, LANES), F32),
            jax.ShapeDtypeStruct((total, width), BF16),
            jax.ShapeDtypeStruct((parts, tall, LANES), BF16),
        ],
    )(core, rows, own, other)


def last_body(full_ref, new_ref, cost_ref):
    parts, tall, _ = full_ref.shape
    children, width = new_ref.shape
    each = children // parts
    for j in range(width // LANES):
        piece = full_ref[:, j * each : (j + 1) * each, :]
        new_ref[:, j * LANES : (j + 1) * LANES] = piece.reshape(children, LANES)
    cost_ref[...] = cost_sum(full_ref[:, tall - EXTRA :, :], children // LANES)


def last(full, children, width):
    return kernel_call(
        last_body,
        "last",
        full.size,
        4 * full.size,
        out_shape=[
            jax.ShapeDtypeStruct((children, width), BF16),
            jax.ShapeDtypeStruct((children // LANES, LANES), F32),
        ],
    )(full)


def squares_of(centroids):
    cent_f = centroids.astype(F32)
    return jnp.sum(cent_f * cent_f, axis=1)[None, :]


def local(embeddings, cluster_key, child_first, child_second, coarse_centroids, fine_centroids):
    n_shard = lax.axis_size(SHARD)
    n_group = lax.axis_size(GROUP)
    rows_dev = embeddings.shape[0]
    children = coarse_centroids.shape[1]
    width = embeddings.shape[1]
    devices = n_shard * n_group
    steps = max(1, devices // 128)
    coarse, fine = coarse_centroids[0], fine_centroids[0]
    core = lax.axis_index("core").astype(jnp.int32)[None]
    group = lax.axis_index(GROUP).astype(jnp.int32)[None]
    shard = lax.axis_index(SHARD).astype(jnp.int32)[None]

    info = jnp.stack(
        [cluster_key[:, 0], child_first, child_second] + [jnp.zeros((rows_dev,), jnp.int32)] * 5
    )
    layout = place(info, embeddings, devices, steps)
    arrived = exchange(layout, ALL)

    rows, partial_one = first_sums(arrived, children, n_group, steps)
    parts_one = exchange(partial_one, GROUP)
    costs_one = margins(rows, rows, coarse, squares_of(coarse), 1, steps)
    copies_one = merge(group, parts_one, coarse, costs_one, lax.axis_size("y"))
    own = exchange(copies_one, "y")
    other = lax.ppermute(own, "core", [(0, 1), (1, 0)])

    coarse_new, coarse_cost, residual, partial_two = second_sums(
        core, rows, own, other, children, n_shard, steps
    )
    parts_two = exchange(partial_two, SHARD)
    costs_two = margins(residual, rows, fine, squares_of(fine), 3, steps)
    copies_two = merge(shard, parts_two, fine, costs_two, n_shard)
    fine_new, fine_cost = last(exchange(copies_two, SHARD), children, width)
    return (
        coarse_new[None],
        fine_new[None],
        coarse_cost.reshape(1, children),
        fine_cost.reshape(1, children),
    )


def solution(mesh):
    torus = Mesh(mesh.devices.reshape(-1, 4, mesh.shape["group"] // 2, 2), ALL)
    placed = (
        P(ALL, None),
        P(ALL, None),
        P(ALL),
        P(ALL),
        P(SHARD, None, None),
        P(GROUP, None, None),
    )
    return jax.shard_map(
        local,
        mesh=torus,
        in_specs=placed,
        out_specs=(
            P(SHARD, None, None),
            P(GROUP, None, None),
            P(SHARD, None),
            P(GROUP, None),
        ),
        check_vma=False,
    )
```

```python
import functools

import jax
import jax.numpy as jnp
from jax import lax
from jax.experimental import pallas as pl
from jax.experimental.pallas import tpu as pltpu
from jax.sharding import Mesh
from jax.sharding import PartitionSpec as P

SHARD = ("z", "x")
GROUP = ("y", "core")
ALL = SHARD + GROUP
SWAP = [(0, 1), (1, 0)]
SLOTS = 2
LANES = 128
EXTRA = 16
DIGIT = 16
F32 = jnp.float32
BF16 = jnp.bfloat16


def exchange(blocks, axes):
    return lax.all_to_all(blocks, axes, split_axis=0, concat_axis=0, tiled=True)


def iota(shape, dim):
    return lax.broadcasted_iota(jnp.int32, shape, dim)


def matmul(a, b, dims):
    return lax.dot_general(a, b, (dims, ((), ())), preferred_element_type=F32)


def kernel_call(body, name, flops, moved, **rest):
    return pl.pallas_call(
        body,
        name=name,
        cost_estimate=pl.CostEstimate(flops=flops, bytes_accessed=moved, transcendentals=0),
        compiler_params=pltpu.CompilerParams(vmem_limit_bytes=24 * 2**20),
        **rest,
    )


def whole(shape):
    return pl.BlockSpec(shape, lambda *_: (0,) * len(shape))


def place_body(info_ref, emb_ref, out_ref, wide_ref, place_ref):
    count, width = emb_ref.shape
    devices, slots, wide = out_ref.shape
    step = pl.program_id(0)

    @pl.when(step == 0)
    def _():
        info = info_ref[...]
        turned = jnp.transpose(info.astype(F32)).astype(jnp.int32)
        keys_row, keys_col = info[0:1, :], turned[:, 0:1]
        earlier = (keys_col == keys_row) & (iota((count, count), 0) < iota((count, count), 1))
        rank = jnp.sum(earlier.astype(jnp.int32), axis=0, keepdims=True)
        place_ref[...] = jnp.broadcast_to(keys_row * slots + rank, place_ref.shape)
        one, two = turned[:, 1:2], turned[:, 2:3]
        lane = iota((count, LANES), 1)
        codes = jnp.where(lane == 0, 1, 0)
        for index, value in enumerate((one // DIGIT, one % DIGIT, two // DIGIT, two % DIGIT)):
            codes = jnp.where(lane == index + 1, value, codes)
        wide_ref[:, :width] = emb_ref[...]
        wide_ref[:, width:] = codes.astype(F32).astype(BF16)

    block = devices * slots
    target = iota((block, count), 0) + step * block
    move = (target == place_ref[0:1, :]).astype(F32).astype(BF16)
    moved = matmul(move, wide_ref[...], ((1,), (0,))).astype(BF16)
    out_ref[...] = moved.reshape(devices, slots, wide)


def place(info, embeddings, devices, steps):
    count, width = embeddings.shape
    wide = width + LANES
    each = devices // steps
    return kernel_call(
        place_body,
        "place",
        2 * devices * SLOTS * count * wide,
        2 * (count * width + devices * SLOTS * wide),
        grid=(steps,),
        in_specs=[whole(info.shape), whole(embeddings.shape)],
        out_specs=pl.BlockSpec((each, SLOTS, wide), lambda i: (i, 0, 0)),
        out_shape=jax.ShapeDtypeStruct((devices, SLOTS, wide), BF16),
        scratch_shapes=[pltpu.VMEM((count, wide), BF16), pltpu.VMEM((8, count), jnp.int32)],
    )(info, embeddings)


def label_row(tail, first):
    turned = jnp.transpose(tail.astype(F32))
    label = turned[first : first + 1, :] * DIGIT + turned[first + 1 : first + 2, :]
    return jnp.where(turned[0:1, :] > 0, label, -1.0).astype(jnp.int32)


def label_col(tail, first):
    tail = tail.astype(F32)
    label = tail[:, first : first + 1] * DIGIT + tail[:, first + 1 : first + 2]
    return jnp.where(tail[:, 0:1] > 0, label, -1.0).astype(jnp.int32)


def add_sums(step, rows, label, sums_ref, counts_ref):
    children, count = sums_ref.shape[0], rows.shape[0]
    member = (iota((children, count), 0) == label).astype(F32).astype(BF16)
    sums = matmul(member, rows, ((1,), (0,)))
    counts = matmul(jnp.ones((EXTRA, count), BF16), member, ((1,), (1,)))

    @pl.when(step == 0)
    def _():
        sums_ref[...] = sums
        counts_ref[...] = counts

    @pl.when(step > 0)
    def _():
        sums_ref[...] += sums
        counts_ref[...] += counts


def write_blocks(out_ref, sums_ref, counts_ref):
    parts, tall, _ = out_ref.shape
    children, width = sums_ref.shape
    each = children // parts
    for j in range(width // LANES):
        piece = sums_ref[:, j * LANES : (j + 1) * LANES].astype(BF16)
        out_ref[:, j * each : (j + 1) * each, :] = piece.reshape(parts, each, LANES)
    counts = counts_ref[...].astype(BF16)
    for h in range(parts):
        chunk = h * each // LANES * LANES
        out_ref[h, tall - EXTRA :, :] = counts[:, chunk : chunk + LANES]


def write_halves(core, keep_ref, send_ref, sums_ref, counts_ref):
    parts, tall, _ = keep_ref.shape
    children, width = sums_ref.shape
    each = children // (2 * parts)
    even = core == 0
    for j in range(width // LANES):
        rows = slice(j * each, (j + 1) * each)
        piece = sums_ref[:, j * LANES : (j + 1) * LANES].reshape(parts, 2, each, LANES)
        keep_ref[:, rows, :] = jnp.where(even, piece[:, 0], piece[:, 1]).astype(BF16)
        send_ref[:, rows, :] = jnp.where(even, piece[:, 1], piece[:, 0]).astype(BF16)
    for y in range(parts):
        chunks = [(2 * y + side) * each // LANES * LANES for side in range(2)]
        zero, one = [counts_ref[:, chunk : chunk + LANES] for chunk in chunks]
        keep_ref[y, tall - EXTRA :, :] = jnp.where(even, zero, one).astype(BF16)
        send_ref[y, tall - EXTRA :, :] = jnp.where(even, one, zero).astype(BF16)


def first_body(core_ref, arrived_ref, rows_ref, keep_ref, send_ref, sums_ref, counts_ref):
    count, wide = rows_ref.shape
    step = pl.program_id(0)
    rows = arrived_ref[...].reshape(count, wide)
    rows_ref[...] = rows
    width = wide - LANES
    add_sums(step, rows[:, :width], label_row(rows[:, width:], 1), sums_ref, counts_ref)

    @pl.when(step == pl.num_programs(0) - 1)
    def _():
        write_halves(core_ref[0], keep_ref, send_ref, sums_ref, counts_ref)


def first_sums(core, arrived, children, parts, steps):
    devices, slots, wide = arrived.shape
    width = wide - LANES
    total = devices * slots
    half = (parts // 2, children // parts * (width // LANES) + EXTRA, LANES)
    return kernel_call(
        first_body,
        "first_sums",
        2 * total * children * width,
        4 * total * wide + 2 * children * width,
        grid_spec=pltpu.PrefetchScalarGridSpec(
            num_scalar_prefetch=1,
            grid=(steps,),
            in_specs=[pl.BlockSpec((devices // steps, slots, wide), lambda i, core: (i, 0, 0))],
            out_specs=[
                pl.BlockSpec((total // steps, wide), lambda i, core: (i, 0)),
                whole(half),
                whole(half),
            ],
            scratch_shapes=[
                pltpu.VMEM((children, width), F32),
                pltpu.VMEM((EXTRA, children), F32),
            ],
        ),
        out_shape=[
            jax.ShapeDtypeStruct((total, wide), BF16),
            jax.ShapeDtypeStruct(half, BF16),
            jax.ShapeDtypeStruct(half, BF16),
        ],
    )(core, arrived)


def margin_body(first, rows_ref, tail_ref, cents_ref, squares_ref, out_ref, costs_ref):
    step = pl.program_id(0)
    products = matmul(rows_ref[...], cents_ref[...], ((1,), (1,)))
    scores = squares_ref[...] - 2.0 * products
    member = iota(scores.shape, 1) == label_col(tail_ref[...], first)
    assigned = jnp.sum(jnp.where(member, scores, 0.0), axis=1, keepdims=True)
    margin = assigned - jnp.min(scores, axis=1, keepdims=True)
    costs = jnp.sum(jnp.where(member, margin, 0.0), axis=0, keepdims=True)

    @pl.when(step == 0)
    def _():
        costs_ref[...] = jnp.broadcast_to(costs, costs_ref.shape)

    @pl.when(step > 0)
    def _():
        costs_ref[...] += jnp.broadcast_to(costs, costs_ref.shape)

    @pl.when(step == pl.num_programs(0) - 1)
    def _():
        costs = costs_ref[0:1, :]
        high = costs.astype(BF16).astype(F32)
        chunks = costs.shape[1] // LANES
        index = iota(out_ref.shape, 0)
        out = jnp.zeros(out_ref.shape, F32)
        for q in range(chunks):
            lanes = slice(q * LANES, (q + 1) * LANES)
            out = jnp.where(index == q, high[:, lanes], out)
            out = jnp.where(index == q + chunks, (costs - high)[:, lanes], out)
        out_ref[...] = out.astype(BF16)


def margins(rows, codes, centroids, squares, first, steps):
    total = rows.shape[0]
    children, width = centroids.shape
    tail_at = codes.shape[1] // LANES - 1
    return kernel_call(
        functools.partial(margin_body, first),
        "margins",
        2 * total * children * width,
        2 * (total + children) * width,
        grid=(steps,),
        in_specs=[
            pl.BlockSpec((total // steps, width), lambda i: (i, 0)),
            pl.BlockSpec((total // steps, LANES), lambda i: (i, tail_at)),
            whole(centroids.shape),
            whole(squares.shape),
        ],
        out_specs=whole((EXTRA, LANES)),
        out_shape=jax.ShapeDtypeStruct((EXTRA, LANES), BF16),
        scratch_shapes=[pltpu.VMEM((8, children), F32)],
    )(rows, codes, centroids, squares)


def merge_body(mine_ref, arrived_ref, old_ref, costs_ref, out_ref):
    copies, tall, _ = out_ref.shape
    each, width = old_ref.shape
    total = jnp.sum(arrived_ref[...].astype(F32), axis=0)
    counts = total[tall - EXTRA : tall - EXTRA + 1, :]
    start = lax.rem(mine_ref[0] * each, LANES)
    mask = iota((each, LANES), 1) == iota((each, LANES), 0) + start
    count = jnp.sum(jnp.where(mask, counts, 0.0), axis=1, keepdims=True)
    for j in range(width // LANES):
        old = old_ref[:, j * LANES : (j + 1) * LANES].astype(F32)
        fresh = (total[j * each : (j + 1) * each, :] + old) / (count + 1.0)
        out_ref[:, j * each : (j + 1) * each, :] = jnp.broadcast_to(
            fresh.astype(BF16)[None], (copies, each, LANES)
        )
    out_ref[:, tall - EXTRA :, :] = jnp.broadcast_to(costs_ref[...][None], (copies, EXTRA, LANES))


def merge(mine, arrived, centroids, costs, copies):
    tall = arrived.shape[1]
    width = centroids.shape[1]
    each = (tall - EXTRA) // (width // LANES)
    return kernel_call(
        merge_body,
        "merge",
        arrived.size,
        2 * (arrived.size + each * width + copies * tall * LANES),
        grid_spec=pltpu.PrefetchScalarGridSpec(
            num_scalar_prefetch=1,
            grid=(1,),
            in_specs=[
                pl.BlockSpec(arrived.shape, lambda i, mine: (0, 0, 0)),
                pl.BlockSpec((each, width), lambda i, mine: (mine[0], 0)),
                pl.BlockSpec(costs.shape, lambda i, mine: (0, 0)),
            ],
            out_specs=pl.BlockSpec((copies, tall, LANES), lambda i, mine: (0, 0, 0)),
        ),
        out_shape=jax.ShapeDtypeStruct((copies, tall, LANES), BF16),
    )(mine, arrived, centroids, costs)


def cost_sum(costs, chunks):
    total = jnp.sum(costs.astype(F32), axis=0)
    return total[0:chunks, :] + total[chunks : 2 * chunks, :]


def second_body(
    core_ref, rows_ref, own_ref, other_ref, new_ref, cost_ref, residual_ref, out_ref, sums_ref, counts_ref
):
    step = pl.program_id(0)
    parts, tall, _ = own_ref.shape
    children, width = new_ref.shape
    each = children // (2 * parts)

    @pl.when(step == 0)
    def _():
        core = core_ref[0]
        for ref, side in ((own_ref, core), (other_ref, 1 - core)):
            for y in range(parts):
                at = pl.ds(pl.multiple_of((2 * y + side) * each, each), each)
                for j in range(width // LANES):
                    new_ref[at, j * LANES : (j + 1) * LANES] = ref[y, j * each : (j + 1) * each, :]
        chunks = children // LANES
        cost_ref[...] = cost_sum(own_ref[:, tall - EXTRA :, :], chunks) + cost_sum(
            other_ref[:, tall - EXTRA :, :], chunks
        )

    rows = rows_ref[:, :width]
    tail = rows_ref[:, width:]
    count = rows.shape[0]
    picked = (iota((count, children), 1) == label_col(tail, 1)).astype(F32).astype(BF16)
    center = matmul(picked, new_ref[...], ((1,), (0,)))
    residual = (rows.astype(F32) - center).astype(BF16)
    residual_ref[...] = residual
    add_sums(step, residual, label_row(tail, 3), sums_ref, counts_ref)

    @pl.when(step == pl.num_programs(0) - 1)
    def _():
        write_blocks(out_ref, sums_ref, counts_ref)


def second_sums(core, rows, own, other, children, parts, steps):
    total, wide = rows.shape
    width = wide - LANES
    tall = children // parts * (width // LANES) + EXTRA
    chunks = children // LANES
    return kernel_call(
        second_body,
        "second_sums",
        4 * total * children * width,
        4 * total * wide + 6 * children * width,
        grid_spec=pltpu.PrefetchScalarGridSpec(
            num_scalar_prefetch=1,
            grid=(steps,),
            in_specs=[
                pl.BlockSpec((total // steps, wide), lambda i, core: (i, 0)),
                whole(own.shape),
                whole(other.shape),
            ],
            out_specs=[
                whole((children, width)),
                whole((chunks, LANES)),
                pl.BlockSpec((total // steps, width), lambda i, core: (i, 0)),
                whole((parts, tall, LANES)),
            ],
            scratch_shapes=[
                pltpu.VMEM((children, width), F32),
                pltpu.VMEM((EXTRA, children), F32),
            ],
        ),
        out_shape=[
            jax.ShapeDtypeStruct((children, width), BF16),
            jax.ShapeDtypeStruct((chunks, LANES), F32),
            jax.ShapeDtypeStruct((total, width), BF16),
            jax.ShapeDtypeStruct((parts, tall, LANES), BF16),
        ],
    )(core, rows, own, other)


def last_body(full_ref, new_ref, cost_ref):
    parts, tall, _ = full_ref.shape
    children, width = new_ref.shape
    each = children // parts
    for j in range(width // LANES):
        piece = full_ref[:, j * each : (j + 1) * each, :]
        new_ref[:, j * LANES : (j + 1) * LANES] = piece.reshape(children, LANES)
    cost_ref[...] = cost_sum(full_ref[:, tall - EXTRA :, :], children // LANES)


def last(full, children, width):
    return kernel_call(
        last_body,
        "last",
        full.size,
        4 * full.size,
        out_shape=[
            jax.ShapeDtypeStruct((children, width), BF16),
            jax.ShapeDtypeStruct((children // LANES, LANES), F32),
        ],
    )(full)


def squares_of(centroids):
    cent_f = centroids.astype(F32)
    return jnp.sum(cent_f * cent_f, axis=1)[None, :]


def local(embeddings, cluster_key, child_first, child_second, coarse_centroids, fine_centroids):
    n_shard = lax.axis_size(SHARD)
    n_group = lax.axis_size(GROUP)
    rows_dev = embeddings.shape[0]
    children = coarse_centroids.shape[1]
    width = embeddings.shape[1]
    devices = n_shard * n_group
    steps = max(1, devices // 128)
    coarse, fine = coarse_centroids[0], fine_centroids[0]
    core = lax.axis_index("core").astype(jnp.int32)[None]
    group = lax.axis_index(GROUP).astype(jnp.int32)[None]
    shard = lax.axis_index(SHARD).astype(jnp.int32)[None]

    info = jnp.stack(
        [cluster_key[:, 0], child_first, child_second] + [jnp.zeros((rows_dev,), jnp.int32)] * 5
    )
    layout = place(info, embeddings, devices, steps)
    arrived = exchange(layout, ALL)

    rows, keep, send = first_sums(core, arrived, children, n_group, steps)
    taken = lax.ppermute(send, "core", SWAP)
    parts_one = exchange((keep.astype(F32) + taken.astype(F32)).astype(BF16), "y")
    costs_one = margins(rows, rows, coarse, squares_of(coarse), 1, steps)
    copies_one = merge(group, parts_one, coarse, costs_one, lax.axis_size("y"))
    own = exchange(copies_one, "y")
    other = lax.ppermute(own, "core", SWAP)

    coarse_new, coarse_cost, residual, partial_two = second_sums(
        core, rows, own, other, children, n_shard, steps
    )
    parts_two = exchange(partial_two, SHARD)
    costs_two = margins(residual, rows, fine, squares_of(fine), 3, steps)
    copies_two = merge(shard, parts_two, fine, costs_two, n_shard)
    fine_new, fine_cost = last(exchange(copies_two, SHARD), children, width)
    return (
        coarse_new[None],
        fine_new[None],
        coarse_cost.reshape(1, children),
        fine_cost.reshape(1, children),
    )


def solution(mesh):
    torus = Mesh(mesh.devices.reshape(-1, 4, mesh.shape["group"] // 2, 2), ALL)
    placed = (
        P(ALL, None),
        P(ALL, None),
        P(ALL),
        P(ALL),
        P(SHARD, None, None),
        P(GROUP, None, None),
    )
    return jax.shard_map(
        local,
        mesh=torus,
        in_specs=placed,
        out_specs=(
            P(SHARD, None, None),
            P(GROUP, None, None),
            P(SHARD, None),
            P(GROUP, None),
        ),
        check_vma=False,
    )
```

```python
import jax
import jax.numpy as jnp
from jax import lax
from jax.experimental import pallas as pl
from jax.experimental.pallas import tpu as pltpu
from jax.sharding import Mesh
from jax.sharding import PartitionSpec as P

SHARD = ("z", "x")
GROUP = ("y", "core")
ALL = SHARD + GROUP
SWAP = [(0, 1), (1, 0)]
SLOTS = 2
LANES = 128
EXTRA = 8
PIECES = 2
VMEM_BYTES = 32 * 2**20
DIGIT = 16
F32 = jnp.float32
BF16 = jnp.bfloat16


def exchange(blocks, axes):
    return lax.all_to_all(blocks, axes, split_axis=0, concat_axis=0, tiled=True)


def iota(shape, dim):
    return lax.broadcasted_iota(jnp.int32, shape, dim)


def matmul(a, b, dims):
    return lax.dot_general(a, b, (dims, ((), ())), preferred_element_type=F32)


def kernel_call(body, name, flops, outs, args, scalars=0, scratch=()):
    moved = sum(x.size * x.dtype.itemsize for x in list(outs) + list(args))
    specs = [pl.BlockSpec(memory_space=pltpu.SMEM)] * scalars
    specs += [pl.BlockSpec(memory_space=pltpu.VMEM)] * (len(args) - scalars)
    return pl.pallas_call(
        body,
        name=name,
        in_specs=specs,
        out_specs=[pl.BlockSpec(memory_space=pltpu.VMEM)] * len(outs),
        out_shape=list(outs),
        scratch_shapes=list(scratch),
        cost_estimate=pl.CostEstimate(flops=flops, bytes_accessed=moved, transcendentals=0),
        compiler_params=pltpu.CompilerParams(vmem_limit_bytes=VMEM_BYTES),
    )(*args)


def shaped(shape, dtype=BF16):
    return jax.ShapeDtypeStruct(shape, dtype)


def one_hot(mask):
    return mask.astype(F32).astype(BF16)


def place_body(info_ref, emb_ref, out_ref, wide_ref):
    count, width = emb_ref.shape
    devices, slots, wide = out_ref.shape
    info = info_ref[...]
    turned = jnp.transpose(info.astype(F32)).astype(jnp.int32)
    keys_row, keys_col = info[0:1, :], turned[:, 0:1]
    earlier = (keys_col == keys_row) & (iota((count, count), 0) < iota((count, count), 1))
    rank = jnp.sum(earlier.astype(jnp.int32), axis=0, keepdims=True)
    target = keys_row * slots + rank
    one, two = turned[:, 1:2], turned[:, 2:3]
    lane = iota((count, LANES), 1)
    codes = jnp.where(lane == 0, 1, 0)
    for index, value in enumerate((one // DIGIT, one % DIGIT, two // DIGIT, two % DIGIT)):
        codes = jnp.where(lane == index + 1, value, codes)
    wide_ref[:, :width] = emb_ref[...]
    wide_ref[:, width:] = codes.astype(F32).astype(BF16)
    block = devices // PIECES
    for piece in range(PIECES):
        at = iota((block * slots, count), 0) + piece * block * slots
        moved = matmul(one_hot(at == target), wide_ref[...], ((1,), (0,))).astype(BF16)
        out_ref[piece * block : (piece + 1) * block] = moved.reshape(block, slots, wide)


def place(info, embeddings, devices):
    count, width = embeddings.shape
    wide = width + LANES
    return kernel_call(
        place_body,
        "place",
        2 * devices * SLOTS * count * wide,
        [shaped((devices, SLOTS, wide))],
        [info, embeddings],
        scratch=[pltpu.VMEM((count, wide), BF16)],
    )[0]


def label_row(tail, first):
    turned = jnp.transpose(tail.astype(F32))
    label = turned[first : first + 1, :] * DIGIT + turned[first + 1 : first + 2, :]
    return jnp.where(turned[0:1, :] > 0, label, -1.0).astype(jnp.int32)


def label_col(tail, first):
    tail = tail.astype(F32)
    label = tail[:, first : first + 1] * DIGIT + tail[:, first + 1 : first + 2]
    return jnp.where(tail[:, 0:1] > 0, label, -1.0).astype(jnp.int32)


def sums_of(rows, label, children):
    count = rows.shape[0]
    member = one_hot(iota((children, count), 0) == label)
    sums = matmul(member, rows, ((1,), (0,)))
    return sums, matmul(jnp.ones((EXTRA, count), BF16), member, ((1,), (1,)))


def first_body(core_ref, arrived_ref, rows_ref, keep_ref, send_ref):
    total, wide = rows_ref.shape
    width = wide - LANES
    parts, tall, _ = keep_ref.shape
    each = (tall - EXTRA) // (width // LANES)
    children = 2 * parts * each
    rows = arrived_ref[...].reshape(total, wide)
    rows_ref[...] = rows
    sums, counts = sums_of(rows[:, :width], label_row(rows[:, width:], 1), children)
    even = core_ref[0] == 0
    for j in range(width // LANES):
        at = slice(j * each, (j + 1) * each)
        piece = sums[:, j * LANES : (j + 1) * LANES].reshape(parts, 2, each, LANES)
        keep_ref[:, at, :] = jnp.where(even, piece[:, 0], piece[:, 1]).astype(BF16)
        send_ref[:, at, :] = jnp.where(even, piece[:, 1], piece[:, 0]).astype(BF16)
    for y in range(parts):
        chunks = [(2 * y + side) * each // LANES * LANES for side in range(2)]
        zero, one = [counts[:, chunk : chunk + LANES] for chunk in chunks]
        keep_ref[y, tall - EXTRA :, :] = jnp.where(even, zero, one).astype(BF16)
        send_ref[y, tall - EXTRA :, :] = jnp.where(even, one, zero).astype(BF16)


def first_sums(core, arrived, children, parts):
    devices, slots, wide = arrived.shape
    width = wide - LANES
    total = devices * slots
    half = (parts // 2, children // parts * (width // LANES) + EXTRA, LANES)
    return kernel_call(
        first_body,
        "first_sums",
        2 * total * children * width,
        [shaped((total, wide)), shaped(half), shaped(half)],
        [core, arrived],
        scalars=1,
    )


def residual_of(rows_ref, centers_ref):
    children, width = centers_ref.shape
    rows, tail = rows_ref[:, :width], rows_ref[:, width:]
    picked = one_hot(iota((rows.shape[0], children), 1) == label_col(tail, 1))
    center = matmul(picked, centers_ref[...], ((1,), (0,)))
    return (rows.astype(F32) - center).astype(BF16)


def write_margins(rows, label, cents_ref, squares_ref, out_ref):
    scores = squares_ref[...] - 2.0 * matmul(rows, cents_ref[...], ((1,), (1,)))
    member = iota(scores.shape, 1) == label
    assigned = jnp.sum(jnp.where(member, scores, 0.0), axis=1, keepdims=True)
    margin = assigned - jnp.min(scores, axis=1, keepdims=True)
    costs = jnp.sum(jnp.where(member, margin, 0.0), axis=0, keepdims=True)
    high = costs.astype(BF16).astype(F32)
    chunks = costs.shape[1] // LANES
    index = iota(out_ref.shape, 0)
    out = jnp.zeros(out_ref.shape, F32)
    for q in range(chunks):
        lanes = slice(q * LANES, (q + 1) * LANES)
        out = jnp.where(index == q, high[:, lanes], out)
        out = jnp.where(index == q + chunks, (costs - high)[:, lanes], out)
    out_ref[...] = out.astype(BF16)


def margins_one_body(rows_ref, cents_ref, squares_ref, out_ref):
    width = cents_ref.shape[1]
    label = label_col(rows_ref[:, width:], 1)
    write_margins(rows_ref[:, :width], label, cents_ref, squares_ref, out_ref)


def margins_two_body(rows_ref, centers_ref, cents_ref, squares_ref, out_ref):
    width = cents_ref.shape[1]
    label = label_col(rows_ref[:, width:], 3)
    write_margins(residual_of(rows_ref, centers_ref), label, cents_ref, squares_ref, out_ref)


def margins(body, rows, *others):
    children, width = others[0].shape
    return kernel_call(
        body,
        "margins",
        2 * (len(others) - 1) * rows.shape[0] * children * width,
        [shaped((EXTRA, LANES))],
        [rows, *others],
    )[0]


def merge_body(mine_ref, arrived_ref, old_ref, costs_ref, out_ref):
    copies, tall, _ = out_ref.shape
    width = old_ref.shape[1]
    each = (tall - EXTRA) // (width // LANES)
    total = jnp.sum(arrived_ref[...].astype(F32), axis=0)
    counts = total[tall - EXTRA : tall - EXTRA + 1, :]
    first = mine_ref[0] * each
    mask = iota((each, LANES), 1) == iota((each, LANES), 0) + lax.rem(first, LANES)
    count = jnp.sum(jnp.where(mask, counts, 0.0), axis=1, keepdims=True)
    old_all = old_ref[pl.ds(pl.multiple_of(first, each), each), :].astype(F32)
    for j in range(width // LANES):
        old = old_all[:, j * LANES : (j + 1) * LANES]
        fresh = (total[j * each : (j + 1) * each, :] + old) / (count + 1.0)
        out_ref[:, j * each : (j + 1) * each, :] = jnp.broadcast_to(
            fresh.astype(BF16)[None], (copies, each, LANES)
        )
    out_ref[:, tall - EXTRA :, :] = jnp.broadcast_to(costs_ref[...][None], (copies, EXTRA, LANES))


def merge(mine, arrived, centroids, costs, copies):
    return kernel_call(
        merge_body,
        "merge",
        arrived.size,
        [shaped((copies,) + arrived.shape[1:])],
        [mine, arrived, centroids, costs],
        scalars=1,
    )[0]


def cost_sum(costs, chunks):
    total = jnp.sum(costs.astype(F32), axis=0)
    return total[0:chunks, :] + total[chunks : 2 * chunks, :]


def second_body(core_ref, rows_ref, own_ref, other_ref, new_ref, cost_ref, out_ref):
    parts, tall, _ = own_ref.shape
    children, width = new_ref.shape
    each = children // (2 * parts)
    core = core_ref[0]
    for ref, side in ((own_ref, core), (other_ref, 1 - core)):
        for y in range(parts):
            at = pl.ds(pl.multiple_of((2 * y + side) * each, each), each)
            for j in range(width // LANES):
                new_ref[at, j * LANES : (j + 1) * LANES] = ref[y, j * each : (j + 1) * each, :]
    chunks = children // LANES
    cost_ref[...] = cost_sum(own_ref[:, tall - EXTRA :, :], chunks) + cost_sum(
        other_ref[:, tall - EXTRA :, :], chunks
    )
    label = label_row(rows_ref[:, width:], 3)
    sums, counts = sums_of(residual_of(rows_ref, new_ref), label, children)
    parts, tall, _ = out_ref.shape
    each = children // parts
    for j in range(width // LANES):
        piece = sums[:, j * LANES : (j + 1) * LANES].astype(BF16)
        out_ref[:, j * each : (j + 1) * each, :] = piece.reshape(parts, each, LANES)
    for h in range(parts):
        chunk = h * each // LANES * LANES
        out_ref[h, tall - EXTRA :, :] = counts[:, chunk : chunk + LANES].astype(BF16)


def second_sums(core, rows, own, other, children, parts):
    total, wide = rows.shape
    width = wide - LANES
    tall = children // parts * (width // LANES) + EXTRA
    return kernel_call(
        second_body,
        "second_sums",
        4 * total * children * width,
        [
            shaped((children, width)),
            shaped((children // LANES, LANES), F32),
            shaped((parts, tall, LANES)),
        ],
        [core, rows, own, other],
        scalars=1,
    )


def last_body(full_ref, new_ref, cost_ref):
    parts, tall, _ = full_ref.shape
    children, width = new_ref.shape
    each = children // parts
    for j in range(width // LANES):
        piece = full_ref[:, j * each : (j + 1) * each, :]
        new_ref[:, j * LANES : (j + 1) * LANES] = piece.reshape(children, LANES)
    cost_ref[...] = cost_sum(full_ref[:, tall - EXTRA :, :], children // LANES)


def last(full, children, width):
    return kernel_call(
        last_body,
        "last",
        full.size,
        [shaped((children, width)), shaped((children // LANES, LANES), F32)],
        [full],
    )


def squares_of(centroids):
    cent_f = centroids.astype(F32)
    return jnp.sum(cent_f * cent_f, axis=1)[None, :]


def local(embeddings, cluster_key, child_first, child_second, coarse_centroids, fine_centroids):
    n_shard = lax.axis_size(SHARD)
    n_group = lax.axis_size(GROUP)
    rows_dev = embeddings.shape[0]
    children = coarse_centroids.shape[1]
    width = embeddings.shape[1]
    devices = n_shard * n_group
    coarse, fine = coarse_centroids[0], fine_centroids[0]
    core = lax.axis_index("core").astype(jnp.int32)[None]
    group = lax.axis_index(GROUP).astype(jnp.int32)[None]
    shard = lax.axis_index(SHARD).astype(jnp.int32)[None]

    info = jnp.stack(
        [cluster_key[:, 0], child_first, child_second] + [jnp.zeros((rows_dev,), jnp.int32)] * 5
    )
    layout = place(info, embeddings, devices)
    layout, core, group, shard = lax.optimization_barrier((layout, core, group, shard))
    arrived = exchange(layout, ALL)

    rows, keep, send = first_sums(core, arrived, children, n_group)
    taken = lax.ppermute(send, "core", SWAP)
    parts_one = exchange((keep.astype(F32) + taken.astype(F32)).astype(BF16), "y")
    costs_one = margins(margins_one_body, rows, coarse, squares_of(coarse))
    copies_one = merge(group, parts_one, coarse, costs_one, lax.axis_size("y"))
    own = exchange(copies_one, "y")
    other = lax.ppermute(own, "core", SWAP)

    coarse_new, coarse_cost, partial_two = second_sums(core, rows, own, other, children, n_shard)
    parts_two = exchange(partial_two, SHARD)
    costs_two = margins(margins_two_body, rows, coarse_new, fine, squares_of(fine))
    copies_two = merge(shard, parts_two, fine, costs_two, n_shard)
    fine_new, fine_cost = last(exchange(copies_two, SHARD), children, width)
    return (
        coarse_new[None],
        fine_new[None],
        coarse_cost.reshape(1, children),
        fine_cost.reshape(1, children),
    )


def solution(mesh):
    torus = Mesh(mesh.devices.reshape(-1, 4, mesh.shape["group"] // 2, 2), ALL)
    placed = (
        P(ALL, None),
        P(ALL, None),
        P(ALL),
        P(ALL),
        P(SHARD, None, None),
        P(GROUP, None, None),
    )
    return jax.shard_map(
        local,
        mesh=torus,
        in_specs=placed,
        out_specs=(
            P(SHARD, None, None),
            P(GROUP, None, None),
            P(SHARD, None),
            P(GROUP, None),
        ),
        check_vma=False,
    )
```

```python
import jax
import jax.numpy as jnp
from jax import lax
from jax.experimental import pallas as pl
from jax.experimental.pallas import tpu as pltpu
from jax.sharding import Mesh
from jax.sharding import PartitionSpec as P

SHARD = ("z", "x")
GROUP = ("y", "core")
ALL = SHARD + GROUP
SWAP = [(0, 1), (1, 0)]
SLOTS = 2
LANES = 128
EXTRA = 8
PIECES = 2
VMEM_BYTES = 32 * 2**20
DIGIT = 16
F32 = jnp.float32
BF16 = jnp.bfloat16


def exchange(blocks, axes):
    return lax.all_to_all(blocks, axes, split_axis=0, concat_axis=0, tiled=True)


def iota(shape, dim):
    return lax.broadcasted_iota(jnp.int32, shape, dim)


def matmul(a, b, dims):
    return lax.dot_general(a, b, (dims, ((), ())), preferred_element_type=F32)


def kernel_call(body, name, flops, outs, args, scalars=0, scratch=()):
    moved = sum(x.size * x.dtype.itemsize for x in list(outs) + list(args))
    specs = [pl.BlockSpec(memory_space=pltpu.SMEM)] * scalars
    specs += [pl.BlockSpec(memory_space=pltpu.VMEM)] * (len(args) - scalars)
    return pl.pallas_call(
        body,
        name=name,
        in_specs=specs,
        out_specs=[pl.BlockSpec(memory_space=pltpu.VMEM)] * len(outs),
        out_shape=list(outs),
        scratch_shapes=list(scratch),
        cost_estimate=pl.CostEstimate(flops=flops, bytes_accessed=moved, transcendentals=0),
        compiler_params=pltpu.CompilerParams(vmem_limit_bytes=VMEM_BYTES),
    )(*args)


def shaped(shape, dtype=BF16):
    return jax.ShapeDtypeStruct(shape, dtype)


def one_hot(mask):
    return mask.astype(F32).astype(BF16)


def place_body(info_ref, emb_ref, out_ref, wide_ref):
    count, width = emb_ref.shape
    devices, slots, wide = out_ref.shape
    info = info_ref[...]
    turned = jnp.transpose(info.astype(F32)).astype(jnp.int32)
    keys_row, keys_col = info[0:1, :], turned[:, 0:1]
    earlier = (keys_col == keys_row) & (iota((count, count), 0) < iota((count, count), 1))
    rank = jnp.sum(earlier.astype(jnp.int32), axis=0, keepdims=True)
    target = keys_row * slots + rank
    one, two = turned[:, 1:2], turned[:, 2:3]
    lane = iota((count, LANES), 1)
    codes = jnp.where(lane == 0, 1, 0)
    for index, value in enumerate((one // DIGIT, one % DIGIT, two // DIGIT, two % DIGIT)):
        codes = jnp.where(lane == index + 1, value, codes)
    wide_ref[:, :width] = emb_ref[...]
    wide_ref[:, width:] = codes.astype(F32).astype(BF16)
    block = devices // PIECES
    for piece in range(PIECES):
        at = iota((block * slots, count), 0) + piece * block * slots
        moved = matmul(one_hot(at == target), wide_ref[...], ((1,), (0,))).astype(BF16)
        out_ref[piece * block : (piece + 1) * block] = moved.reshape(block, slots, wide)


def place(info, embeddings, devices):
    count, width = embeddings.shape
    wide = width + LANES
    return kernel_call(
        place_body,
        "place",
        2 * devices * SLOTS * count * wide,
        [shaped((devices, SLOTS, wide))],
        [info, embeddings],
        scratch=[pltpu.VMEM((count, wide), BF16)],
    )[0]


def label_row(tail, first):
    turned = jnp.transpose(tail.astype(F32))
    label = turned[first : first + 1, :] * DIGIT + turned[first + 1 : first + 2, :]
    return jnp.where(turned[0:1, :] > 0, label, -1.0).astype(jnp.int32)


def label_col(tail, first):
    tail = tail.astype(F32)
    label = tail[:, first : first + 1] * DIGIT + tail[:, first + 1 : first + 2]
    return jnp.where(tail[:, 0:1] > 0, label, -1.0).astype(jnp.int32)


def sums_of(rows, label, children):
    count = rows.shape[0]
    member = one_hot(iota((children, count), 0) == label)
    sums = matmul(member, rows, ((1,), (0,)))
    return sums, matmul(jnp.ones((EXTRA, count), BF16), member, ((1,), (1,)))


def first_body(core_ref, arrived_ref, rows_ref, keep_ref, send_ref):
    total, wide = rows_ref.shape
    width = wide - LANES
    parts, tall, _ = keep_ref.shape
    each = (tall - EXTRA) // (width // LANES)
    children = 2 * parts * each
    rows = arrived_ref[...].reshape(total, wide)
    rows_ref[...] = rows
    sums, counts = sums_of(rows[:, :width], label_row(rows[:, width:], 1), children)
    even = core_ref[0] == 0
    for j in range(width // LANES):
        at = slice(j * each, (j + 1) * each)
        piece = sums[:, j * LANES : (j + 1) * LANES].reshape(parts, 2, each, LANES)
        keep_ref[:, at, :] = jnp.where(even, piece[:, 0], piece[:, 1]).astype(BF16)
        send_ref[:, at, :] = jnp.where(even, piece[:, 1], piece[:, 0]).astype(BF16)
    for y in range(parts):
        chunks = [(2 * y + side) * each // LANES * LANES for side in range(2)]
        zero, one = [counts[:, chunk : chunk + LANES] for chunk in chunks]
        keep_ref[y, tall - EXTRA :, :] = jnp.where(even, zero, one).astype(BF16)
        send_ref[y, tall - EXTRA :, :] = jnp.where(even, one, zero).astype(BF16)


def first_sums(core, arrived, children, parts):
    devices, slots, wide = arrived.shape
    width = wide - LANES
    total = devices * slots
    half = (parts // 2, children // parts * (width // LANES) + EXTRA, LANES)
    return kernel_call(
        first_body,
        "first_sums",
        2 * total * children * width,
        [shaped((total, wide)), shaped(half), shaped(half)],
        [core, arrived],
        scalars=1,
    )


def residual_of(rows_ref, centers_ref):
    children, width = centers_ref.shape
    rows, tail = rows_ref[:, :width], rows_ref[:, width:]
    picked = one_hot(iota((rows.shape[0], children), 1) == label_col(tail, 1))
    center = matmul(picked, centers_ref[...], ((1,), (0,)))
    return (rows.astype(F32) - center).astype(BF16)


def write_margins(rows, label, cents_ref, squares_ref, out_ref):
    scores = squares_ref[...] - 2.0 * matmul(rows, cents_ref[...], ((1,), (1,)))
    member = iota(scores.shape, 1) == label
    assigned = jnp.sum(jnp.where(member, scores, 0.0), axis=1, keepdims=True)
    margin = assigned - jnp.min(scores, axis=1, keepdims=True)
    costs = jnp.sum(jnp.where(member, margin, 0.0), axis=0, keepdims=True)
    high = costs.astype(BF16).astype(F32)
    chunks = costs.shape[1] // LANES
    index = iota(out_ref.shape, 0)
    out = jnp.zeros(out_ref.shape, F32)
    for q in range(chunks):
        lanes = slice(q * LANES, (q + 1) * LANES)
        out = jnp.where(index == q, high[:, lanes], out)
        out = jnp.where(index == q + chunks, (costs - high)[:, lanes], out)
    out_ref[...] = out.astype(BF16)


def margins_one_body(rows_ref, cents_ref, squares_ref, out_ref):
    width = cents_ref.shape[1]
    label = label_col(rows_ref[:, width:], 1)
    write_margins(rows_ref[:, :width], label, cents_ref, squares_ref, out_ref)


def margins_two_body(rows_ref, centers_ref, cents_ref, squares_ref, out_ref):
    width = cents_ref.shape[1]
    label = label_col(rows_ref[:, width:], 3)
    write_margins(residual_of(rows_ref, centers_ref), label, cents_ref, squares_ref, out_ref)


def margins(body, rows, *others):
    children, width = others[0].shape
    return kernel_call(
        body,
        "margins",
        2 * (len(others) - 1) * rows.shape[0] * children * width,
        [shaped((EXTRA, LANES))],
        [rows, *others],
    )[0]


def merge_body(mine_ref, arrived_ref, old_ref, costs_ref, out_ref):
    copies, tall, _ = out_ref.shape
    width = old_ref.shape[1]
    each = (tall - EXTRA) // (width // LANES)
    total = jnp.sum(arrived_ref[...].astype(F32), axis=0)
    counts = total[tall - EXTRA : tall - EXTRA + 1, :]
    first = mine_ref[0] * each
    mask = iota((each, LANES), 1) == iota((each, LANES), 0) + lax.rem(first, LANES)
    count = jnp.sum(jnp.where(mask, counts, 0.0), axis=1, keepdims=True)
    old_all = old_ref[pl.ds(pl.multiple_of(first, each), each), :].astype(F32)
    for j in range(width // LANES):
        old = old_all[:, j * LANES : (j + 1) * LANES]
        fresh = (total[j * each : (j + 1) * each, :] + old) / (count + 1.0)
        out_ref[:, j * each : (j + 1) * each, :] = jnp.broadcast_to(
            fresh.astype(BF16)[None], (copies, each, LANES)
        )
    out_ref[:, tall - EXTRA :, :] = jnp.broadcast_to(costs_ref[...][None], (copies, EXTRA, LANES))


def merge(mine, arrived, centroids, costs, copies):
    return kernel_call(
        merge_body,
        "merge",
        arrived.size,
        [shaped((copies,) + arrived.shape[1:])],
        [mine, arrived, centroids, costs],
        scalars=1,
    )[0]


def cost_sum(costs, chunks):
    total = jnp.sum(costs.astype(F32), axis=0)
    return total[0:chunks, :] + total[chunks : 2 * chunks, :]


def second_body(core_ref, rows_ref, own_ref, other_ref, new_ref, cost_ref, out_ref):
    parts, tall, _ = own_ref.shape
    children, width = new_ref.shape
    each = children // (2 * parts)
    core = core_ref[0]
    for ref, side in ((own_ref, core), (other_ref, 1 - core)):
        for y in range(parts):
            at = pl.ds(pl.multiple_of((2 * y + side) * each, each), each)
            for j in range(width // LANES):
                new_ref[at, j * LANES : (j + 1) * LANES] = ref[y, j * each : (j + 1) * each, :]
    chunks = children // LANES
    cost_ref[...] = cost_sum(own_ref[:, tall - EXTRA :, :], chunks) + cost_sum(
        other_ref[:, tall - EXTRA :, :], chunks
    )
    label = label_row(rows_ref[:, width:], 3)
    sums, counts = sums_of(residual_of(rows_ref, new_ref), label, children)
    nx, nz, tall, _ = out_ref.shape
    each = children // (nx * nz)
    for j in range(width // LANES):
        piece = sums[:, j * LANES : (j + 1) * LANES].astype(BF16).reshape(nz, nx, each, LANES)
        for x in range(nx):
            out_ref[x, :, j * each : (j + 1) * each, :] = piece[:, x]
    for z in range(nz):
        for x in range(nx):
            chunk = (z * nx + x) * each // LANES * LANES
            out_ref[x, z, tall - EXTRA :, :] = counts[:, chunk : chunk + LANES].astype(BF16)


def second_sums(core, rows, own, other, children, nx, nz):
    total, wide = rows.shape
    width = wide - LANES
    tall = children // (nx * nz) * (width // LANES) + EXTRA
    return kernel_call(
        second_body,
        "second_sums",
        4 * total * children * width,
        [
            shaped((children, width)),
            shaped((children // LANES, LANES), F32),
            shaped((nx, nz, tall, LANES)),
        ],
        [core, rows, own, other],
        scalars=1,
    )


def last_body(full_ref, new_ref, cost_ref):
    nx, nz, tall, _ = full_ref.shape
    children, width = new_ref.shape
    each = children // (nx * nz)
    for j in range(width // LANES):
        piece = [full_ref[x, :, j * each : (j + 1) * each, :] for x in range(nx)]
        new_ref[:, j * LANES : (j + 1) * LANES] = jnp.stack(piece, axis=1).reshape(children, LANES)
    chunks = children // LANES
    cost_ref[...] = sum(cost_sum(full_ref[x, :, tall - EXTRA :, :], chunks) for x in range(nx))


def last(full, children, width):
    return kernel_call(
        last_body,
        "last",
        full.size,
        [shaped((children, width)), shaped((children // LANES, LANES), F32)],
        [full],
    )


def squares_of(centroids):
    cent_f = centroids.astype(F32)
    return jnp.sum(cent_f * cent_f, axis=1)[None, :]


def local(embeddings, cluster_key, child_first, child_second, coarse_centroids, fine_centroids):
    n_shard = lax.axis_size(SHARD)
    n_group = lax.axis_size(GROUP)
    rows_dev = embeddings.shape[0]
    children = coarse_centroids.shape[1]
    width = embeddings.shape[1]
    devices = n_shard * n_group
    coarse, fine = coarse_centroids[0], fine_centroids[0]
    core = lax.axis_index("core").astype(jnp.int32)[None]
    group = lax.axis_index(GROUP).astype(jnp.int32)[None]
    shard = lax.axis_index(SHARD).astype(jnp.int32)[None]

    info = jnp.stack(
        [cluster_key[:, 0], child_first, child_second] + [jnp.zeros((rows_dev,), jnp.int32)] * 5
    )
    layout = place(info, embeddings, devices)
    layout, core, group, shard = lax.optimization_barrier((layout, core, group, shard))
    arrived = exchange(layout, ALL)

    rows, keep, send = first_sums(core, arrived, children, n_group)
    taken = lax.ppermute(send, "core", SWAP)
    parts_one = exchange((keep.astype(F32) + taken.astype(F32)).astype(BF16), "y")
    costs_one = margins(margins_one_body, rows, coarse, squares_of(coarse))
    copies_one = merge(group, parts_one, coarse, costs_one, lax.axis_size("y"))
    own = exchange(copies_one, "y")
    other = lax.ppermute(own, "core", SWAP)

    nx, nz = lax.axis_size("x"), lax.axis_size("z")
    coarse_new, coarse_cost, partial_two = second_sums(core, rows, own, other, children, nx, nz)
    parts_two = jnp.sum(exchange(partial_two, "x").astype(F32), axis=0).astype(BF16)
    parts_two = exchange(parts_two, "z")
    costs_two = margins(margins_two_body, rows, coarse_new, fine, squares_of(fine))
    copies_two = exchange(merge(shard, parts_two, fine, costs_two, nz), "z")
    full_two = exchange(jnp.broadcast_to(copies_two[None], (nx,) + copies_two.shape), "x")
    fine_new, fine_cost = last(full_two, children, width)
    return (
        coarse_new[None],
        fine_new[None],
        coarse_cost.reshape(1, children),
        fine_cost.reshape(1, children),
    )


def solution(mesh):
    torus = Mesh(mesh.devices.reshape(-1, 4, mesh.shape["group"] // 2, 2), ALL)
    placed = (
        P(ALL, None),
        P(ALL, None),
        P(ALL),
        P(ALL),
        P(SHARD, None, None),
        P(GROUP, None, None),
    )
    return jax.shard_map(
        local,
        mesh=torus,
        in_specs=placed,
        out_specs=(
            P(SHARD, None, None),
            P(GROUP, None, None),
            P(SHARD, None),
            P(GROUP, None),
        ),
        check_vma=False,
    )
```

```python
import jax
import jax.numpy as jnp
from jax import lax
from jax.experimental import pallas as pl
from jax.experimental.pallas import tpu as pltpu
from jax.sharding import Mesh
from jax.sharding import PartitionSpec as P

SHARD = ("z", "x")
GROUP = ("y", "core")
ALL = SHARD + GROUP
SWAP = [(0, 1), (1, 0)]
SLOTS = 2
LANES = 128
EXTRA = 8
PIECES = 2
VMEM_BYTES = 32 * 2**20
DIGIT = 16
F32 = jnp.float32
BF16 = jnp.bfloat16


def exchange(blocks, axes):
    return lax.all_to_all(blocks, axes, split_axis=0, concat_axis=0, tiled=True)


def mirrored(blocks, axes, outer):
    n = lax.axis_size(axes[0])
    low = lax.axis_size(axes[1:]) // outer
    groups = []
    for index in range(outer):
        base = index * low
        groups.append([i * outer * low + base for i in range(n)])
        groups.append([(n - 1 - i) * outer * low + base + 1 for i in range(n)])
    return lax.all_to_all(
        blocks, axes, split_axis=0, concat_axis=0, tiled=True, axis_index_groups=groups
    )


def mirror(index, count, core):
    return index + core * (count - 1 - 2 * index)


def iota(shape, dim):
    return lax.broadcasted_iota(jnp.int32, shape, dim)


def matmul(a, b, dims):
    return lax.dot_general(a, b, (dims, ((), ())), preferred_element_type=F32)


def kernel_call(body, name, flops, outs, args, scalars=0, scratch=()):
    moved = sum(x.size * x.dtype.itemsize for x in list(outs) + list(args))
    specs = [pl.BlockSpec(memory_space=pltpu.SMEM)] * scalars
    specs += [pl.BlockSpec(memory_space=pltpu.VMEM)] * (len(args) - scalars)
    return pl.pallas_call(
        body,
        name=name,
        in_specs=specs,
        out_specs=[pl.BlockSpec(memory_space=pltpu.VMEM)] * len(outs),
        out_shape=list(outs),
        scratch_shapes=list(scratch),
        cost_estimate=pl.CostEstimate(flops=flops, bytes_accessed=moved, transcendentals=0),
        compiler_params=pltpu.CompilerParams(vmem_limit_bytes=VMEM_BYTES),
    )(*args)


def shaped(shape, dtype=BF16):
    return jax.ShapeDtypeStruct(shape, dtype)


def one_hot(mask):
    return mask.astype(F32).astype(BF16)


def place_body(keys_ref, one_ref, two_ref, emb_ref, out_ref, wide_ref):
    count, width = emb_ref.shape
    devices, slots, wide = out_ref.shape
    info = jnp.concatenate(
        [keys_ref[...], one_ref[...], two_ref[...], jnp.zeros((5, count), jnp.int32)], axis=0
    )
    turned = jnp.transpose(info.astype(F32)).astype(jnp.int32)
    keys_row, keys_col = info[0:1, :], turned[:, 0:1]
    earlier = (keys_col == keys_row) & (iota((count, count), 0) < iota((count, count), 1))
    rank = jnp.sum(earlier.astype(jnp.int32), axis=0, keepdims=True)
    target = keys_row * slots + rank
    one, two = turned[:, 1:2], turned[:, 2:3]
    lane = iota((count, LANES), 1)
    codes = jnp.where(lane == 0, 1, 0)
    for index, value in enumerate((one // DIGIT, one % DIGIT, two // DIGIT, two % DIGIT)):
        codes = jnp.where(lane == index + 1, value, codes)
    wide_ref[:, :width] = emb_ref[...]
    wide_ref[:, width:] = codes.astype(F32).astype(BF16)
    block = devices // PIECES
    for piece in range(PIECES):
        at = iota((block * slots, count), 0) + piece * block * slots
        moved = matmul(one_hot(at == target), wide_ref[...], ((1,), (0,))).astype(BF16)
        out_ref[piece * block : (piece + 1) * block] = moved.reshape(block, slots, wide)


def place(keys, one, two, embeddings, devices):
    count, width = embeddings.shape
    wide = width + LANES
    return kernel_call(
        place_body,
        "place",
        2 * devices * SLOTS * count * wide,
        [shaped((devices, SLOTS, wide))],
        [keys, one, two, embeddings],
        scratch=[pltpu.VMEM((count, wide), BF16)],
    )[0]


def label_row(tail, first):
    turned = jnp.transpose(tail.astype(F32))
    label = turned[first : first + 1, :] * DIGIT + turned[first + 1 : first + 2, :]
    return jnp.where(turned[0:1, :] > 0, label, -1.0).astype(jnp.int32)


def label_col(tail, first):
    tail = tail.astype(F32)
    label = tail[:, first : first + 1] * DIGIT + tail[:, first + 1 : first + 2]
    return jnp.where(tail[:, 0:1] > 0, label, -1.0).astype(jnp.int32)


def sums_of(rows, label, children):
    count = rows.shape[0]
    member = one_hot(iota((children, count), 0) == label)
    sums = matmul(member, rows, ((1,), (0,)))
    return sums, matmul(jnp.ones((EXTRA, count), BF16), member, ((1,), (1,)))


def rows_of(arrived_ref):
    devices, slots, wide = arrived_ref.shape
    rows = arrived_ref[...].reshape(devices * slots, wide)
    return rows[:, : wide - LANES], rows[:, wide - LANES :]


def first_body(core_ref, arrived_ref, keep_ref, send_ref):
    rows, tail = rows_of(arrived_ref)
    width = rows.shape[1]
    parts, tall, _ = keep_ref.shape
    each = (tall - EXTRA) // (width // LANES)
    children = 2 * parts * each
    sums, counts = sums_of(rows, label_row(tail, 1), children)
    even = core_ref[0] == 0
    for j in range(width // LANES):
        at = slice(j * each, (j + 1) * each)
        piece = sums[:, j * LANES : (j + 1) * LANES].reshape(parts, 2, each, LANES)
        for y in range(parts):
            zero, one = piece[y, 0], piece[parts - 1 - y, 1]
            keep_ref[y, at, :] = jnp.where(even, zero, one).astype(BF16)
            send_ref[y, at, :] = jnp.where(even, one, zero).astype(BF16)
    for y in range(parts):
        blocks = (2 * y, 2 * (parts - 1 - y) + 1)
        chunks = [block * each // LANES * LANES for block in blocks]
        zero, one = [counts[:, chunk : chunk + LANES] for chunk in chunks]
        keep_ref[y, tall - EXTRA :, :] = jnp.where(even, zero, one).astype(BF16)
        send_ref[y, tall - EXTRA :, :] = jnp.where(even, one, zero).astype(BF16)


def first_sums(core, arrived, children, parts):
    devices, slots, wide = arrived.shape
    width = wide - LANES
    total = devices * slots
    half = (parts // 2, children // parts * (width // LANES) + EXTRA, LANES)
    return kernel_call(
        first_body,
        "first_sums",
        2 * total * children * width,
        [shaped(half), shaped(half)],
        [core, arrived],
        scalars=1,
    )


def residual_of(rows, tail, centers_ref):
    children = centers_ref.shape[0]
    picked = one_hot(iota((rows.shape[0], children), 1) == label_col(tail, 1))
    center = matmul(picked, centers_ref[...], ((1,), (0,)))
    return (rows.astype(F32) - center).astype(BF16)


def write_margins(rows, label, cents_ref, squares_ref, out_ref):
    scores = squares_ref[...] - 2.0 * matmul(rows, cents_ref[...], ((1,), (1,)))
    member = iota(scores.shape, 1) == label
    assigned = jnp.sum(jnp.where(member, scores, 0.0), axis=1, keepdims=True)
    margin = assigned - jnp.min(scores, axis=1, keepdims=True)
    costs = jnp.sum(jnp.where(member, margin, 0.0), axis=0, keepdims=True)
    high = costs.astype(BF16).astype(F32)
    chunks = costs.shape[1] // LANES
    index = iota(out_ref.shape, 0)
    out = jnp.zeros(out_ref.shape, F32)
    for q in range(chunks):
        lanes = slice(q * LANES, (q + 1) * LANES)
        out = jnp.where(index == q, high[:, lanes], out)
        out = jnp.where(index == q + chunks, (costs - high)[:, lanes], out)
    out_ref[...] = out.astype(BF16)


def margins_one_body(arrived_ref, cents_ref, squares_ref, out_ref, rows_ref):
    rows, tail = rows_of(arrived_ref)
    rows_ref[:, : rows.shape[1]] = rows
    rows_ref[:, rows.shape[1] :] = tail
    write_margins(rows, label_col(tail, 1), cents_ref, squares_ref, out_ref)


def margins_two_body(rows_ref, centers_ref, cents_ref, squares_ref, out_ref):
    width = cents_ref.shape[1]
    rows, tail = rows_ref[:, :width], rows_ref[:, width:]
    residual = residual_of(rows, tail, centers_ref)
    write_margins(residual, label_col(tail, 3), cents_ref, squares_ref, out_ref)


def margins_one(arrived, centroids, squares):
    devices, slots, wide = arrived.shape
    return kernel_call(
        margins_one_body,
        "margins_one",
        2 * devices * slots * centroids.size,
        [shaped((EXTRA, LANES)), shaped((devices * slots, wide))],
        [arrived, centroids, squares],
    )


def margins_two(rows, centers, centroids, squares):
    return kernel_call(
        margins_two_body,
        "margins_two",
        4 * rows.shape[0] * centroids.size,
        [shaped((EXTRA, LANES))],
        [rows, centers, centroids, squares],
    )[0]


def merge_body(mine_ref, arrived_ref, old_ref, costs_ref, out_ref):
    copies, tall, _ = out_ref.shape
    width = old_ref.shape[1]
    each = (tall - EXTRA) // (width // LANES)
    total = jnp.sum(arrived_ref[...].astype(F32), axis=0)
    counts = total[tall - EXTRA : tall - EXTRA + 1, :]
    first = mine_ref[0] * each
    mask = iota((each, LANES), 1) == iota((each, LANES), 0) + lax.rem(first, LANES)
    count = jnp.sum(jnp.where(mask, counts, 0.0), axis=1, keepdims=True)
    old_all = old_ref[pl.ds(pl.multiple_of(first, each), each), :].astype(F32)
    for j in range(width // LANES):
        old = old_all[:, j * LANES : (j + 1) * LANES]
        fresh = (total[j * each : (j + 1) * each, :] + old) / (count + 1.0)
        out_ref[:, j * each : (j + 1) * each, :] = jnp.broadcast_to(
            fresh.astype(BF16)[None], (copies, each, LANES)
        )
    out_ref[:, tall - EXTRA :, :] = jnp.broadcast_to(costs_ref[...][None], (copies, EXTRA, LANES))


def merge(mine, arrived, centroids, costs, copies):
    return kernel_call(
        merge_body,
        "merge",
        arrived.size,
        [shaped((copies,) + arrived.shape[1:])],
        [mine, arrived, centroids, costs],
        scalars=1,
    )[0]


def cost_sum(costs, chunks):
    total = jnp.sum(costs.astype(F32), axis=0)
    return total[0:chunks, :] + total[chunks : 2 * chunks, :]


def second_body(core_ref, rows_ref, own_ref, other_ref, new_ref, cost_ref, out_ref):
    parts, tall, _ = own_ref.shape
    children, width = new_ref.shape
    each = children // (2 * parts)
    core = core_ref[0]
    for ref, side in ((own_ref, core), (other_ref, 1 - core)):
        for y in range(parts):
            block = 2 * mirror(y, parts, side) + side
            at = pl.ds(pl.multiple_of(block * each, each), each)
            for j in range(width // LANES):
                new_ref[at, j * LANES : (j + 1) * LANES] = ref[y, j * each : (j + 1) * each, :]
    chunks = children // LANES
    cost_ref[...] = cost_sum(own_ref[:, tall - EXTRA :, :], chunks) + cost_sum(
        other_ref[:, tall - EXTRA :, :], chunks
    )
    rows, tail = rows_ref[:, :width], rows_ref[:, width:]
    sums, counts = sums_of(residual_of(rows, tail, new_ref), label_row(tail, 3), children)
    nx, nz, tall, _ = out_ref.shape
    each = children // (nx * nz)
    for j in range(width // LANES):
        piece = sums[:, j * LANES : (j + 1) * LANES].astype(BF16).reshape(nz, nx, each, LANES)
        for x in range(nx):
            out_ref[mirror(x, nx, core), :, j * each : (j + 1) * each, :] = piece[:, x]
    for z in range(nz):
        for x in range(nx):
            chunk = (z * nx + x) * each // LANES * LANES
            out_ref[mirror(x, nx, core), z, tall - EXTRA :, :] = counts[
                :, chunk : chunk + LANES
            ].astype(BF16)


def second_sums(core, rows, own, other, children, nx, nz):
    total, wide = rows.shape
    width = wide - LANES
    tall = children // (nx * nz) * (width // LANES) + EXTRA
    return kernel_call(
        second_body,
        "second_sums",
        4 * total * children * width,
        [
            shaped((children, width)),
            shaped((children // LANES, LANES), F32),
            shaped((nx, nz, tall, LANES)),
        ],
        [core, rows, own, other],
        scalars=1,
    )


def last_body(core_ref, full_ref, new_ref, cost_ref):
    nx, nz, tall, _ = full_ref.shape
    children, width = new_ref.shape
    each = children // (nx * nz)
    for x in range(nx):
        for z in range(nz):
            block = z * nx + mirror(x, nx, core_ref[0])
            at = pl.ds(pl.multiple_of(block * each, each), each)
            for j in range(width // LANES):
                lanes = slice(j * LANES, (j + 1) * LANES)
                new_ref[at, lanes] = full_ref[x, z, j * each : (j + 1) * each, :]
    chunks = children // LANES
    cost_ref[...] = sum(cost_sum(full_ref[x, :, tall - EXTRA :, :], chunks) for x in range(nx))


def last(core, full, children, width):
    return kernel_call(
        last_body,
        "last",
        full.size,
        [shaped((children, width)), shaped((children // LANES, LANES), F32)],
        [core, full],
        scalars=1,
    )


def squares_of(centroids):
    cent_f = centroids.astype(F32)
    return jnp.sum(cent_f * cent_f, axis=1)[None, :]


def local(embeddings, cluster_key, child_first, child_second, coarse_centroids, fine_centroids):
    n_shard = lax.axis_size(SHARD)
    n_group = lax.axis_size(GROUP)
    rows_dev = embeddings.shape[0]
    children = coarse_centroids.shape[1]
    width = embeddings.shape[1]
    devices = n_shard * n_group
    coarse, fine = coarse_centroids[0], fine_centroids[0]
    core = lax.axis_index("core").astype(jnp.int32)[None]
    group = lax.axis_index(GROUP).astype(jnp.int32)[None]
    shard = lax.axis_index(SHARD).astype(jnp.int32)[None]

    layout = place(
        cluster_key.reshape(1, rows_dev),
        child_first.reshape(1, rows_dev),
        child_second.reshape(1, rows_dev),
        embeddings,
        devices,
    )
    layout, core, group, shard = lax.optimization_barrier((layout, core, group, shard))
    arrived = exchange(layout, ALL)

    keep, send = first_sums(core, arrived, children, n_group)
    taken = lax.ppermute(send, "core", SWAP)
    parts_one = mirrored((keep.astype(F32) + taken.astype(F32)).astype(BF16), GROUP, 1)
    costs_one, rows = margins_one(arrived, coarse, squares_of(coarse))
    copies_one = merge(group, parts_one, coarse, costs_one, lax.axis_size("y"))
    own = mirrored(copies_one, GROUP, 1)
    other = lax.ppermute(own, "core", SWAP)

    nx, nz = lax.axis_size("x"), lax.axis_size("z")
    coarse_new, coarse_cost, partial_two = second_sums(core, rows, own, other, children, nx, nz)
    parts_two = jnp.sum(mirrored(partial_two, ("x",) + GROUP, n_group // 2).astype(F32), axis=0).astype(BF16)
    parts_two = exchange(parts_two, "z")
    costs_two = margins_two(rows, coarse_new, fine, squares_of(fine))
    copies_two = exchange(merge(shard, parts_two, fine, costs_two, nz), "z")
    full_two = jnp.broadcast_to(copies_two[None], (nx,) + copies_two.shape)
    full_two = mirrored(full_two, ("x",) + GROUP, n_group // 2)
    fine_new, fine_cost = last(core, full_two, children, width)
    return (
        coarse_new[None],
        fine_new[None],
        coarse_cost.reshape(1, children),
        fine_cost.reshape(1, children),
    )


def solution(mesh):
    torus = Mesh(mesh.devices.reshape(-1, 4, mesh.shape["group"] // 2, 2), ALL)
    placed = (
        P(ALL, None),
        P(ALL, None),
        P(ALL),
        P(ALL),
        P(SHARD, None, None),
        P(GROUP, None, None),
    )
    return jax.shard_map(
        local,
        mesh=torus,
        in_specs=placed,
        out_specs=(
            P(SHARD, None, None),
            P(GROUP, None, None),
            P(SHARD, None),
            P(GROUP, None),
        ),
        check_vma=False,
    )
```

```python
import jax
import jax.numpy as jnp
from jax import lax
from jax.experimental import pallas as pl
from jax.experimental.pallas import tpu as pltpu
from jax.sharding import Mesh
from jax.sharding import PartitionSpec as P

SHARD = ("z", "x")
GROUP = ("y", "core")
ALL = SHARD + GROUP
SWAP = [(0, 1), (1, 0)]
SLOTS = 2
LANES = 128
EXTRA = 8
PIECES = 2
VMEM_BYTES = 32 * 2**20
DIGIT = 16
F32 = jnp.float32
BF16 = jnp.bfloat16


def exchange(blocks, axes):
    return lax.all_to_all(blocks, axes, split_axis=0, concat_axis=0, tiled=True)


def mirrored(blocks):
    n = lax.axis_size("y")
    groups = [[2 * i for i in range(n)], [2 * (n - 1 - i) + 1 for i in range(n)]]
    return lax.all_to_all(
        blocks, GROUP, split_axis=0, concat_axis=0, tiled=True, axis_index_groups=groups
    )


def mirror(index, count, core):
    return index + core * (count - 1 - 2 * index)


def iota(shape, dim):
    return lax.broadcasted_iota(jnp.int32, shape, dim)


def matmul(a, b, dims):
    return lax.dot_general(a, b, (dims, ((), ())), preferred_element_type=F32)


def kernel_call(body, name, flops, outs, args, scalars=0, scratch=()):
    moved = sum(x.size * x.dtype.itemsize for x in list(outs) + list(args))
    specs = [pl.BlockSpec(memory_space=pltpu.SMEM)] * scalars
    specs += [pl.BlockSpec(memory_space=pltpu.VMEM)] * (len(args) - scalars)
    return pl.pallas_call(
        body,
        name=name,
        in_specs=specs,
        out_specs=[pl.BlockSpec(memory_space=pltpu.VMEM)] * len(outs),
        out_shape=list(outs),
        scratch_shapes=list(scratch),
        cost_estimate=pl.CostEstimate(flops=flops, bytes_accessed=moved, transcendentals=0),
        compiler_params=pltpu.CompilerParams(vmem_limit_bytes=VMEM_BYTES),
    )(*args)


def shaped(shape, dtype=BF16):
    return jax.ShapeDtypeStruct(shape, dtype)


def one_hot(mask):
    return mask.astype(F32).astype(BF16)


def place_body(info_ref, emb_ref, out_ref, wide_ref):
    count, width = emb_ref.shape
    devices, slots, wide = out_ref.shape
    info = info_ref[...]
    turned = jnp.transpose(info.astype(F32)).astype(jnp.int32)
    keys_row, keys_col = info[0:1, :], turned[:, 0:1]
    earlier = (keys_col == keys_row) & (iota((count, count), 0) < iota((count, count), 1))
    rank = jnp.sum(earlier.astype(jnp.int32), axis=0, keepdims=True)
    target = keys_row * slots + rank
    one, two = turned[:, 1:2], turned[:, 2:3]
    lane = iota((count, LANES), 1)
    codes = jnp.where(lane == 0, 1, 0)
    for index, value in enumerate((one // DIGIT, one % DIGIT, two // DIGIT, two % DIGIT)):
        codes = jnp.where(lane == index + 1, value, codes)
    wide_ref[:, :width] = emb_ref[...]
    wide_ref[:, width:] = codes.astype(F32).astype(BF16)
    block = devices // PIECES
    for piece in range(PIECES):
        at = iota((block * slots, count), 0) + piece * block * slots
        moved = matmul(one_hot(at == target), wide_ref[...], ((1,), (0,))).astype(BF16)
        out_ref[piece * block : (piece + 1) * block] = moved.reshape(block, slots, wide)


def place(info, embeddings, devices):
    count, width = embeddings.shape
    wide = width + LANES
    return kernel_call(
        place_body,
        "place",
        2 * devices * SLOTS * count * wide,
        [shaped((devices, SLOTS, wide))],
        [info, embeddings],
        scratch=[pltpu.VMEM((count, wide), BF16)],
    )[0]


def label_row(tail, first):
    turned = jnp.transpose(tail.astype(F32))
    label = turned[first : first + 1, :] * DIGIT + turned[first + 1 : first + 2, :]
    return jnp.where(turned[0:1, :] > 0, label, -1.0).astype(jnp.int32)


def label_col(tail, first):
    tail = tail.astype(F32)
    label = tail[:, first : first + 1] * DIGIT + tail[:, first + 1 : first + 2]
    return jnp.where(tail[:, 0:1] > 0, label, -1.0).astype(jnp.int32)


def sums_of(rows, label, children):
    count = rows.shape[0]
    member = one_hot(iota((children, count), 0) == label)
    sums = matmul(member, rows, ((1,), (0,)))
    return sums, matmul(jnp.ones((EXTRA, count), BF16), member, ((1,), (1,)))


def rows_of(arrived_ref):
    devices, slots, wide = arrived_ref.shape
    rows = arrived_ref[...].reshape(devices * slots, wide)
    return rows[:, : wide - LANES], rows[:, wide - LANES :]


def first_body(core_ref, arrived_ref, keep_ref, send_ref):
    rows, tail = rows_of(arrived_ref)
    width = rows.shape[1]
    parts, tall, _ = keep_ref.shape
    each = (tall - EXTRA) // (width // LANES)
    children = 2 * parts * each
    sums, counts = sums_of(rows, label_row(tail, 1), children)
    even = core_ref[0] == 0
    for j in range(width // LANES):
        at = slice(j * each, (j + 1) * each)
        piece = sums[:, j * LANES : (j + 1) * LANES].reshape(parts, 2, each, LANES)
        for y in range(parts):
            zero, one = piece[y, 0], piece[parts - 1 - y, 1]
            keep_ref[y, at, :] = jnp.where(even, zero, one).astype(BF16)
            send_ref[y, at, :] = jnp.where(even, one, zero).astype(BF16)
    for y in range(parts):
        blocks = (2 * y, 2 * (parts - 1 - y) + 1)
        chunks = [block * each // LANES * LANES for block in blocks]
        zero, one = [counts[:, chunk : chunk + LANES] for chunk in chunks]
        keep_ref[y, tall - EXTRA :, :] = jnp.where(even, zero, one).astype(BF16)
        send_ref[y, tall - EXTRA :, :] = jnp.where(even, one, zero).astype(BF16)


def first_sums(core, arrived, children, parts):
    devices, slots, wide = arrived.shape
    width = wide - LANES
    total = devices * slots
    half = (parts // 2, children // parts * (width // LANES) + EXTRA, LANES)
    return kernel_call(
        first_body,
        "first_sums",
        2 * total * children * width,
        [shaped(half), shaped(half)],
        [core, arrived],
        scalars=1,
    )


def residual_of(rows, tail, centers_ref):
    children = centers_ref.shape[0]
    picked = one_hot(iota((rows.shape[0], children), 1) == label_col(tail, 1))
    center = matmul(picked, centers_ref[...], ((1,), (0,)))
    return (rows.astype(F32) - center).astype(BF16)


def write_margins(rows, label, cents_ref, squares_ref, out_ref):
    scores = squares_ref[...] - 2.0 * matmul(rows, cents_ref[...], ((1,), (1,)))
    member = iota(scores.shape, 1) == label
    assigned = jnp.sum(jnp.where(member, scores, 0.0), axis=1, keepdims=True)
    margin = assigned - jnp.min(scores, axis=1, keepdims=True)
    costs = jnp.sum(jnp.where(member, margin, 0.0), axis=0, keepdims=True)
    high = costs.astype(BF16).astype(F32)
    chunks = costs.shape[1] // LANES
    index = iota(out_ref.shape, 0)
    out = jnp.zeros(out_ref.shape, F32)
    for q in range(chunks):
        lanes = slice(q * LANES, (q + 1) * LANES)
        out = jnp.where(index == q, high[:, lanes], out)
        out = jnp.where(index == q + chunks, (costs - high)[:, lanes], out)
    out_ref[...] = out.astype(BF16)


def margins_one_body(arrived_ref, cents_ref, squares_ref, out_ref, rows_ref):
    rows, tail = rows_of(arrived_ref)
    rows_ref[:, : rows.shape[1]] = rows
    rows_ref[:, rows.shape[1] :] = tail
    write_margins(rows, label_col(tail, 1), cents_ref, squares_ref, out_ref)


def margins_two_body(rows_ref, centers_ref, cents_ref, squares_ref, out_ref):
    width = cents_ref.shape[1]
    rows, tail = rows_ref[:, :width], rows_ref[:, width:]
    residual = residual_of(rows, tail, centers_ref)
    write_margins(residual, label_col(tail, 3), cents_ref, squares_ref, out_ref)


def margins_one(arrived, centroids, squares):
    devices, slots, wide = arrived.shape
    return kernel_call(
        margins_one_body,
        "margins_one",
        2 * devices * slots * centroids.size,
        [shaped((EXTRA, LANES)), shaped((devices * slots, wide))],
        [arrived, centroids, squares],
    )


def margins_two(rows, centers, centroids, squares):
    return kernel_call(
        margins_two_body,
        "margins_two",
        4 * rows.shape[0] * centroids.size,
        [shaped((EXTRA, LANES))],
        [rows, centers, centroids, squares],
    )[0]


def merge_body(mine_ref, arrived_ref, old_ref, costs_ref, out_ref):
    copies, tall, _ = out_ref.shape
    width = old_ref.shape[1]
    each = (tall - EXTRA) // (width // LANES)
    total = jnp.sum(arrived_ref[...].astype(F32), axis=0)
    counts = total[tall - EXTRA : tall - EXTRA + 1, :]
    first = mine_ref[0] * each
    mask = iota((each, LANES), 1) == iota((each, LANES), 0) + lax.rem(first, LANES)
    count = jnp.sum(jnp.where(mask, counts, 0.0), axis=1, keepdims=True)
    old_all = old_ref[pl.ds(pl.multiple_of(first, each), each), :].astype(F32)
    for j in range(width // LANES):
        old = old_all[:, j * LANES : (j + 1) * LANES]
        fresh = (total[j * each : (j + 1) * each, :] + old) / (count + 1.0)
        out_ref[:, j * each : (j + 1) * each, :] = jnp.broadcast_to(
            fresh.astype(BF16)[None], (copies, each, LANES)
        )
    out_ref[:, tall - EXTRA :, :] = jnp.broadcast_to(costs_ref[...][None], (copies, EXTRA, LANES))


def merge(mine, arrived, centroids, costs, copies):
    return kernel_call(
        merge_body,
        "merge",
        arrived.size,
        [shaped((copies,) + arrived.shape[1:])],
        [mine, arrived, centroids, costs],
        scalars=1,
    )[0]


def cost_sum(costs, chunks):
    total = jnp.sum(costs.astype(F32), axis=0)
    return total[0:chunks, :] + total[chunks : 2 * chunks, :]


def second_body(core_ref, rows_ref, own_ref, other_ref, new_ref, cost_ref, out_ref):
    parts, tall, _ = own_ref.shape
    children, width = new_ref.shape
    each = children // (2 * parts)
    core = core_ref[0]
    for ref, side in ((own_ref, core), (other_ref, 1 - core)):
        for y in range(parts):
            block = 2 * mirror(y, parts, side) + side
            at = pl.ds(pl.multiple_of(block * each, each), each)
            for j in range(width // LANES):
                new_ref[at, j * LANES : (j + 1) * LANES] = ref[y, j * each : (j + 1) * each, :]
    chunks = children // LANES
    cost_ref[...] = cost_sum(own_ref[:, tall - EXTRA :, :], chunks) + cost_sum(
        other_ref[:, tall - EXTRA :, :], chunks
    )
    rows, tail = rows_ref[:, :width], rows_ref[:, width:]
    sums, counts = sums_of(residual_of(rows, tail, new_ref), label_row(tail, 3), children)
    nx, nz, tall, _ = out_ref.shape
    each = children // (nx * nz)
    for j in range(width // LANES):
        piece = sums[:, j * LANES : (j + 1) * LANES].astype(BF16).reshape(nz, nx, each, LANES)
        for x in range(nx):
            out_ref[x, :, j * each : (j + 1) * each, :] = piece[:, x]
    for z in range(nz):
        for x in range(nx):
            chunk = (z * nx + x) * each // LANES * LANES
            out_ref[x, z, tall - EXTRA :, :] = counts[:, chunk : chunk + LANES].astype(BF16)


def second_sums(core, rows, own, other, children, nx, nz):
    total, wide = rows.shape
    width = wide - LANES
    tall = children // (nx * nz) * (width // LANES) + EXTRA
    return kernel_call(
        second_body,
        "second_sums",
        4 * total * children * width,
        [
            shaped((children, width)),
            shaped((children // LANES, LANES), F32),
            shaped((nx, nz, tall, LANES)),
        ],
        [core, rows, own, other],
        scalars=1,
    )


def last_body(full_ref, new_ref, cost_ref):
    nx, nz, tall, _ = full_ref.shape
    children, width = new_ref.shape
    each = children // (nx * nz)
    for x in range(nx):
        for z in range(nz):
            at = slice((z * nx + x) * each, (z * nx + x + 1) * each)
            for j in range(width // LANES):
                lanes = slice(j * LANES, (j + 1) * LANES)
                new_ref[at, lanes] = full_ref[x, z, j * each : (j + 1) * each, :]
    chunks = children // LANES
    cost_ref[...] = sum(cost_sum(full_ref[x, :, tall - EXTRA :, :], chunks) for x in range(nx))


def last(full, children, width):
    return kernel_call(
        last_body,
        "last",
        full.size,
        [shaped((children, width)), shaped((children // LANES, LANES), F32)],
        [full],
    )


def squares_of(centroids):
    cent_f = centroids.astype(F32)
    return jnp.sum(cent_f * cent_f, axis=1)[None, :]


def local(embeddings, cluster_key, child_first, child_second, coarse_centroids, fine_centroids):
    n_shard = lax.axis_size(SHARD)
    n_group = lax.axis_size(GROUP)
    rows_dev = embeddings.shape[0]
    children = coarse_centroids.shape[1]
    width = embeddings.shape[1]
    devices = n_shard * n_group
    coarse, fine = coarse_centroids[0], fine_centroids[0]
    core = lax.axis_index("core").astype(jnp.int32)[None]
    group = lax.axis_index(GROUP).astype(jnp.int32)[None]
    shard = lax.axis_index(SHARD).astype(jnp.int32)[None]

    info = jnp.stack(
        [cluster_key[:, 0], child_first, child_second] + [jnp.zeros((rows_dev,), jnp.int32)] * 5
    )
    layout = place(info, embeddings, devices)
    layout, core, group, shard = lax.optimization_barrier((layout, core, group, shard))
    arrived = exchange(layout, ALL)

    keep, send = first_sums(core, arrived, children, n_group)
    taken = lax.ppermute(send, "core", SWAP)
    parts_one = mirrored((keep.astype(F32) + taken.astype(F32)).astype(BF16))
    costs_one, rows = margins_one(arrived, coarse, squares_of(coarse))
    copies_one = merge(group, parts_one, coarse, costs_one, lax.axis_size("y"))
    own = mirrored(copies_one)
    other = lax.ppermute(own, "core", SWAP)

    nx, nz = lax.axis_size("x"), lax.axis_size("z")
    coarse_new, coarse_cost, partial_two = second_sums(core, rows, own, other, children, nx, nz)
    parts_two = jnp.sum(exchange(partial_two, "x").astype(F32), axis=0).astype(BF16)
    parts_two = exchange(parts_two, "z")
    costs_two = margins_two(rows, coarse_new, fine, squares_of(fine))
    copies_two = exchange(merge(shard, parts_two, fine, costs_two, nz), "z")
    full_two = jnp.broadcast_to(copies_two[None], (nx,) + copies_two.shape)
    fine_new, fine_cost = last(exchange(full_two, "x"), children, width)
    return (
        coarse_new[None],
        fine_new[None],
        coarse_cost.reshape(1, children),
        fine_cost.reshape(1, children),
    )


def solution(mesh):
    torus = Mesh(mesh.devices.reshape(-1, 4, mesh.shape["group"] // 2, 2), ALL)
    placed = (
        P(ALL, None),
        P(ALL, None),
        P(ALL),
        P(ALL),
        P(SHARD, None, None),
        P(GROUP, None, None),
    )
    return jax.shard_map(
        local,
        mesh=torus,
        in_specs=placed,
        out_specs=(
            P(SHARD, None, None),
            P(GROUP, None, None),
            P(SHARD, None),
            P(GROUP, None),
        ),
        check_vma=False,
    )
```

```python
import jax
import jax.numpy as jnp
from jax import lax
from jax.experimental import pallas as pl
from jax.experimental.pallas import tpu as pltpu
from jax.sharding import Mesh
from jax.sharding import PartitionSpec as P

SHARD = ("z", "x")
GROUP = ("y", "core")
ALL = SHARD + GROUP
SWAP = [(0, 1), (1, 0)]
SLOTS = 2
LANES = 128
EXTRA = 8
PIECES = 2
VMEM_BYTES = 32 * 2**20
DIGIT = 16
F32 = jnp.float32
BF16 = jnp.bfloat16


def exchange(blocks, axes):
    return lax.all_to_all(blocks, axes, split_axis=0, concat_axis=0, tiled=True)


def mirrored(blocks):
    n = lax.axis_size("y")
    groups = [[2 * i for i in range(n)], [2 * (n - 1 - i) + 1 for i in range(n)]]
    return lax.all_to_all(
        blocks, GROUP, split_axis=0, concat_axis=0, tiled=True, axis_index_groups=groups
    )


def mirror(index, count, core):
    return index + core * (count - 1 - 2 * index)


def iota(shape, dim):
    return lax.broadcasted_iota(jnp.int32, shape, dim)


def matmul(a, b, dims):
    return lax.dot_general(a, b, (dims, ((), ())), preferred_element_type=F32)


def kernel_call(body, name, flops, outs, args, scalars=0, scratch=()):
    moved = sum(x.size * x.dtype.itemsize for x in list(outs) + list(args))
    specs = [pl.BlockSpec(memory_space=pltpu.SMEM)] * scalars
    specs += [pl.BlockSpec(memory_space=pltpu.VMEM)] * (len(args) - scalars)
    return pl.pallas_call(
        body,
        name=name,
        in_specs=specs,
        out_specs=[pl.BlockSpec(memory_space=pltpu.VMEM)] * len(outs),
        out_shape=list(outs),
        scratch_shapes=list(scratch),
        cost_estimate=pl.CostEstimate(flops=flops, bytes_accessed=moved, transcendentals=0),
        compiler_params=pltpu.CompilerParams(vmem_limit_bytes=VMEM_BYTES),
    )(*args)


def shaped(shape, dtype=BF16):
    return jax.ShapeDtypeStruct(shape, dtype)


def one_hot(mask):
    return mask.astype(F32).astype(BF16)


def place_body(info_ref, emb_ref, out_ref, wide_ref):
    count, width = emb_ref.shape
    devices, slots, wide = out_ref.shape
    info = info_ref[...]
    turned = jnp.transpose(info.astype(F32)).astype(jnp.int32)
    keys_row, keys_col = info[0:1, :], turned[:, 0:1]
    earlier = (keys_col == keys_row) & (iota((count, count), 0) < iota((count, count), 1))
    rank = jnp.sum(earlier.astype(jnp.int32), axis=0, keepdims=True)
    target = keys_row * slots + rank
    one, two = turned[:, 1:2], turned[:, 2:3]
    lane = iota((count, LANES), 1)
    codes = jnp.where(lane == 0, 1, 0)
    for index, value in enumerate((one // DIGIT, one % DIGIT, two // DIGIT, two % DIGIT)):
        codes = jnp.where(lane == index + 1, value, codes)
    wide_ref[:, :width] = emb_ref[...]
    wide_ref[:, width:] = codes.astype(F32).astype(BF16)
    block = devices // PIECES
    for piece in range(PIECES):
        at = iota((block * slots, count), 0) + piece * block * slots
        moved = matmul(one_hot(at == target), wide_ref[...], ((1,), (0,))).astype(BF16)
        out_ref[piece * block : (piece + 1) * block] = moved.reshape(block, slots, wide)


def place(info, embeddings, devices):
    count, width = embeddings.shape
    wide = width + LANES
    return kernel_call(
        place_body,
        "place",
        2 * devices * SLOTS * count * wide,
        [shaped((devices, SLOTS, wide))],
        [info, embeddings],
        scratch=[pltpu.VMEM((count, wide), BF16)],
    )[0]


def label_row(tail, first):
    turned = jnp.transpose(tail.astype(F32))
    label = turned[first : first + 1, :] * DIGIT + turned[first + 1 : first + 2, :]
    return jnp.where(turned[0:1, :] > 0, label, -1.0).astype(jnp.int32)


def label_col(tail, first):
    tail = tail.astype(F32)
    label = tail[:, first : first + 1] * DIGIT + tail[:, first + 1 : first + 2]
    return jnp.where(tail[:, 0:1] > 0, label, -1.0).astype(jnp.int32)


def sums_of(rows, label, children):
    count = rows.shape[0]
    member = one_hot(iota((children, count), 0) == label)
    sums = matmul(member, rows, ((1,), (0,)))
    return sums, matmul(jnp.ones((EXTRA, count), BF16), member, ((1,), (1,)))


def rows_of(arrived_ref):
    devices, slots, wide = arrived_ref.shape
    rows = arrived_ref[...].reshape(devices * slots, wide)
    return rows[:, : wide - LANES], rows[:, wide - LANES :]


def first_body(core_ref, arrived_ref, keep_ref, send_ref):
    rows, tail = rows_of(arrived_ref)
    width = rows.shape[1]
    parts, tall, _ = keep_ref.shape
    each = (tall - EXTRA) // (width // LANES)
    children = 2 * parts * each
    sums, counts = sums_of(rows, label_row(tail, 1), children)
    even = core_ref[0] == 0
    for j in range(width // LANES):
        at = slice(j * each, (j + 1) * each)
        piece = sums[:, j * LANES : (j + 1) * LANES].reshape(parts, 2, each, LANES)
        for y in range(parts):
            zero, one = piece[y, 0], piece[parts - 1 - y, 1]
            keep_ref[y, at, :] = jnp.where(even, zero, one).astype(BF16)
            send_ref[y, at, :] = jnp.where(even, one, zero).astype(BF16)
    for y in range(parts):
        blocks = (2 * y, 2 * (parts - 1 - y) + 1)
        chunks = [block * each // LANES * LANES for block in blocks]
        zero, one = [counts[:, chunk : chunk + LANES] for chunk in chunks]
        keep_ref[y, tall - EXTRA :, :] = jnp.where(even, zero, one).astype(BF16)
        send_ref[y, tall - EXTRA :, :] = jnp.where(even, one, zero).astype(BF16)


def first_sums(core, arrived, children, parts):
    devices, slots, wide = arrived.shape
    width = wide - LANES
    total = devices * slots
    half = (parts // 2, children // parts * (width // LANES) + EXTRA, LANES)
    return kernel_call(
        first_body,
        "first_sums",
        2 * total * children * width,
        [shaped(half), shaped(half)],
        [core, arrived],
        scalars=1,
    )


def residual_of(rows, tail, centers_ref):
    children = centers_ref.shape[0]
    picked = one_hot(iota((rows.shape[0], children), 1) == label_col(tail, 1))
    center = matmul(picked, centers_ref[...], ((1,), (0,)))
    return (rows.astype(F32) - center).astype(BF16)


def write_margins(rows, label, cents_ref, squares_ref, out_ref):
    scores = squares_ref[...] - 2.0 * matmul(rows, cents_ref[...], ((1,), (1,)))
    member = iota(scores.shape, 1) == label
    assigned = jnp.sum(jnp.where(member, scores, 0.0), axis=1, keepdims=True)
    margin = assigned - jnp.min(scores, axis=1, keepdims=True)
    costs = jnp.sum(jnp.where(member, margin, 0.0), axis=0, keepdims=True)
    high = costs.astype(BF16).astype(F32)
    chunks = costs.shape[1] // LANES
    index = iota(out_ref.shape, 0)
    out = jnp.zeros(out_ref.shape, F32)
    for q in range(chunks):
        lanes = slice(q * LANES, (q + 1) * LANES)
        out = jnp.where(index == q, high[:, lanes], out)
        out = jnp.where(index == q + chunks, (costs - high)[:, lanes], out)
    out_ref[...] = out.astype(BF16)


def margins_one_body(arrived_ref, cents_ref, squares_ref, out_ref, rows_ref):
    rows, tail = rows_of(arrived_ref)
    rows_ref[:, : rows.shape[1]] = rows
    rows_ref[:, rows.shape[1] :] = tail
    write_margins(rows, label_col(tail, 1), cents_ref, squares_ref, out_ref)


def margins_two_body(rows_ref, centers_ref, cents_ref, squares_ref, out_ref):
    width = cents_ref.shape[1]
    rows, tail = rows_ref[:, :width], rows_ref[:, width:]
    residual = residual_of(rows, tail, centers_ref)
    write_margins(residual, label_col(tail, 3), cents_ref, squares_ref, out_ref)


def margins_one(arrived, centroids, squares):
    devices, slots, wide = arrived.shape
    return kernel_call(
        margins_one_body,
        "margins_one",
        2 * devices * slots * centroids.size,
        [shaped((EXTRA, LANES)), shaped((devices * slots, wide))],
        [arrived, centroids, squares],
    )


def margins_two(rows, centers, centroids, squares):
    return kernel_call(
        margins_two_body,
        "margins_two",
        4 * rows.shape[0] * centroids.size,
        [shaped((EXTRA, LANES))],
        [rows, centers, centroids, squares],
    )[0]


def merge_body(mine_ref, arrived_ref, old_ref, costs_ref, out_ref):
    copies, tall, _ = out_ref.shape
    width = old_ref.shape[1]
    each = (tall - EXTRA) // (width // LANES)
    total = jnp.sum(arrived_ref[...].astype(F32), axis=0)
    counts = total[tall - EXTRA : tall - EXTRA + 1, :]
    first = mine_ref[0] * each
    mask = iota((each, LANES), 1) == iota((each, LANES), 0) + lax.rem(first, LANES)
    count = jnp.sum(jnp.where(mask, counts, 0.0), axis=1, keepdims=True)
    old_all = old_ref[pl.ds(pl.multiple_of(first, each), each), :].astype(F32)
    for j in range(width // LANES):
        old = old_all[:, j * LANES : (j + 1) * LANES]
        fresh = (total[j * each : (j + 1) * each, :] + old) / (count + 1.0)
        out_ref[:, j * each : (j + 1) * each, :] = jnp.broadcast_to(
            fresh.astype(BF16)[None], (copies, each, LANES)
        )
    out_ref[:, tall - EXTRA :, :] = jnp.broadcast_to(costs_ref[...][None], (copies, EXTRA, LANES))


def merge(mine, arrived, centroids, costs, copies):
    return kernel_call(
        merge_body,
        "merge",
        arrived.size,
        [shaped((copies,) + arrived.shape[1:])],
        [mine, arrived, centroids, costs],
        scalars=1,
    )[0]


def cost_sum(costs, chunks):
    total = jnp.sum(costs.astype(F32), axis=0)
    return total[0:chunks, :] + total[chunks : 2 * chunks, :]


def second_body(core_ref, rows_ref, own_ref, other_ref, new_ref, cost_ref, out_ref):
    parts, tall, _ = own_ref.shape
    children, width = new_ref.shape
    each = children // (2 * parts)
    core = core_ref[0]
    for ref, side in ((own_ref, core), (other_ref, 1 - core)):
        for y in range(parts):
            block = 2 * mirror(y, parts, side) + side
            at = pl.ds(pl.multiple_of(block * each, each), each)
            for j in range(width // LANES):
                new_ref[at, j * LANES : (j + 1) * LANES] = ref[y, j * each : (j + 1) * each, :]
    chunks = children // LANES
    cost_ref[...] = cost_sum(own_ref[:, tall - EXTRA :, :], chunks) + cost_sum(
        other_ref[:, tall - EXTRA :, :], chunks
    )
    rows, tail = rows_ref[:, :width], rows_ref[:, width:]
    sums, counts = sums_of(residual_of(rows, tail, new_ref), label_row(tail, 3), children)
    nx, nz, tall, _ = out_ref.shape
    each = children // (nx * nz)
    for j in range(width // LANES):
        piece = sums[:, j * LANES : (j + 1) * LANES].astype(BF16).reshape(nz, nx, each, LANES)
        for x in range(nx):
            out_ref[x, :, j * each : (j + 1) * each, :] = piece[:, x]
    for z in range(nz):
        for x in range(nx):
            chunk = (z * nx + x) * each // LANES * LANES
            out_ref[x, z, tall - EXTRA :, :] = counts[:, chunk : chunk + LANES].astype(BF16)


def second_sums(core, rows, own, other, children, nx, nz):
    total, wide = rows.shape
    width = wide - LANES
    tall = children // (nx * nz) * (width // LANES) + EXTRA
    return kernel_call(
        second_body,
        "second_sums",
        4 * total * children * width,
        [
            shaped((children, width)),
            shaped((children // LANES, LANES), F32),
            shaped((nx, nz, tall, LANES)),
        ],
        [core, rows, own, other],
        scalars=1,
    )


def last_body(full_ref, new_ref, cost_ref):
    nx, nz, tall, _ = full_ref.shape
    children, width = new_ref.shape
    each = children // (nx * nz)
    for x in range(nx):
        for z in range(nz):
            at = slice((z * nx + x) * each, (z * nx + x + 1) * each)
            for j in range(width // LANES):
                lanes = slice(j * LANES, (j + 1) * LANES)
                new_ref[at, lanes] = full_ref[x, z, j * each : (j + 1) * each, :]
    chunks = children // LANES
    cost_ref[...] = sum(cost_sum(full_ref[x, :, tall - EXTRA :, :], chunks) for x in range(nx))


def last(full, children, width):
    return kernel_call(
        last_body,
        "last",
        full.size,
        [shaped((children, width)), shaped((children // LANES, LANES), F32)],
        [full],
    )


def squares_of(centroids):
    cent_f = centroids.astype(F32)
    return jnp.sum(cent_f * cent_f, axis=1)[None, :]


def local(embeddings, cluster_key, child_first, child_second, coarse_centroids, fine_centroids):
    n_shard = lax.axis_size(SHARD)
    n_group = lax.axis_size(GROUP)
    rows_dev = embeddings.shape[0]
    children = coarse_centroids.shape[1]
    width = embeddings.shape[1]
    devices = n_shard * n_group
    coarse, fine = coarse_centroids[0], fine_centroids[0]
    core = lax.axis_index("core").astype(jnp.int32)[None]
    group = lax.axis_index(GROUP).astype(jnp.int32)[None]
    shard = lax.axis_index(SHARD).astype(jnp.int32)[None]

    info = jnp.stack(
        [cluster_key[:, 0], child_first, child_second] + [jnp.zeros((rows_dev,), jnp.int32)] * 5
    )
    layout = place(info, embeddings, devices)
    layout, core, group, shard = lax.optimization_barrier((layout, core, group, shard))
    arrived = exchange(layout, ALL)

    keep, send = first_sums(core, arrived, children, n_group)
    taken = lax.ppermute(send, "core", SWAP)
    parts_one = mirrored((keep.astype(F32) + taken.astype(F32)).astype(BF16))
    costs_one, rows = margins_one(arrived, coarse, squares_of(coarse))
    copies_one = merge(group, parts_one, coarse, costs_one, lax.axis_size("y"))
    own = mirrored(copies_one)
    other = lax.ppermute(own, "core", SWAP)

    nx, nz = lax.axis_size("x"), lax.axis_size("z")
    coarse_new, coarse_cost, partial_two = second_sums(core, rows, own, other, children, nx, nz)
    parts_two = exchange(partial_two, "x")
    costs_two = margins_two(rows, coarse_new, fine, squares_of(fine))
    parts_two, costs_two = lax.optimization_barrier((parts_two, costs_two))
    parts_two = exchange(jnp.sum(parts_two.astype(F32), axis=0).astype(BF16), "z")
    copies_two = exchange(merge(shard, parts_two, fine, costs_two, nz), "z")
    full_two = jnp.broadcast_to(copies_two[None], (nx,) + copies_two.shape)
    fine_new, fine_cost = last(exchange(full_two, "x"), children, width)
    return (
        coarse_new[None],
        fine_new[None],
        coarse_cost.reshape(1, children),
        fine_cost.reshape(1, children),
    )


def solution(mesh):
    torus = Mesh(mesh.devices.reshape(-1, 4, mesh.shape["group"] // 2, 2), ALL)
    placed = (
        P(ALL, None),
        P(ALL, None),
        P(ALL),
        P(ALL),
        P(SHARD, None, None),
        P(GROUP, None, None),
    )
    return jax.shard_map(
        local,
        mesh=torus,
        in_specs=placed,
        out_specs=(
            P(SHARD, None, None),
            P(GROUP, None, None),
            P(SHARD, None),
            P(GROUP, None),
        ),
        check_vma=False,
    )
```

```python
import jax
import jax.numpy as jnp
from jax import lax
from jax.experimental import pallas as pl
from jax.experimental.pallas import tpu as pltpu
from jax.sharding import Mesh
from jax.sharding import PartitionSpec as P

SHARD = ("z", "x")
GROUP = ("y", "core")
ALL = SHARD + GROUP
SWAP = [(0, 1), (1, 0)]
SLOTS = 2
LANES = 128
EXTRA = 16
PIECES = 2
VMEM_BYTES = 32 * 2**20
DIGIT = 16
F32 = jnp.float32
BF16 = jnp.bfloat16


def exchange(blocks, axes):
    return lax.all_to_all(blocks, axes, split_axis=0, concat_axis=0, tiled=True)


def mirrored(blocks):
    n = lax.axis_size("y")
    groups = [[2 * i for i in range(n)], [2 * (n - 1 - i) + 1 for i in range(n)]]
    return lax.all_to_all(
        blocks, GROUP, split_axis=0, concat_axis=0, tiled=True, axis_index_groups=groups
    )


def mirror(index, count, core):
    return index + core * (count - 1 - 2 * index)


def iota(shape, dim):
    return lax.broadcasted_iota(jnp.int32, shape, dim)


def matmul(a, b, dims):
    return lax.dot_general(a, b, (dims, ((), ())), preferred_element_type=F32)


def kernel_call(body, name, flops, outs, args, scalars=0, scratch=()):
    moved = sum(x.size * x.dtype.itemsize for x in list(outs) + list(args))
    specs = [pl.BlockSpec(memory_space=pltpu.SMEM)] * scalars
    specs += [pl.BlockSpec(memory_space=pltpu.VMEM)] * (len(args) - scalars)
    return pl.pallas_call(
        body,
        name=name,
        in_specs=specs,
        out_specs=[pl.BlockSpec(memory_space=pltpu.VMEM)] * len(outs),
        out_shape=list(outs),
        scratch_shapes=list(scratch),
        cost_estimate=pl.CostEstimate(flops=flops, bytes_accessed=moved, transcendentals=0),
        compiler_params=pltpu.CompilerParams(vmem_limit_bytes=VMEM_BYTES),
    )(*args)


def shaped(shape, dtype=BF16):
    return jax.ShapeDtypeStruct(shape, dtype)


def one_hot(mask):
    return mask.astype(F32).astype(BF16)


def place_body(info_ref, emb_ref, out_ref, wide_ref):
    count, width = emb_ref.shape
    devices, slots, wide = out_ref.shape
    info = info_ref[...]
    turned = jnp.transpose(info.astype(F32)).astype(jnp.int32)
    keys_row, keys_col = info[0:1, :], turned[:, 0:1]
    earlier = (keys_col == keys_row) & (iota((count, count), 0) < iota((count, count), 1))
    rank = jnp.sum(earlier.astype(jnp.int32), axis=0, keepdims=True)
    target = keys_row * slots + rank
    one, two = turned[:, 1:2], turned[:, 2:3]
    lane = iota((count, LANES), 1)
    codes = jnp.where(lane == 0, 1, 0)
    for index, value in enumerate((one // DIGIT, one % DIGIT, two // DIGIT, two % DIGIT)):
        codes = jnp.where(lane == index + 1, value, codes)
    wide_ref[:, :width] = emb_ref[...]
    wide_ref[:, width:] = codes.astype(F32).astype(BF16)
    block = devices // PIECES
    for piece in range(PIECES):
        at = iota((block * slots, count), 0) + piece * block * slots
        moved = matmul(one_hot(at == target), wide_ref[...], ((1,), (0,))).astype(BF16)
        out_ref[piece * block : (piece + 1) * block] = moved.reshape(block, slots, wide)


def place(info, embeddings, devices):
    count, width = embeddings.shape
    wide = width + LANES
    return kernel_call(
        place_body,
        "place",
        2 * devices * SLOTS * count * wide,
        [shaped((devices, SLOTS, wide))],
        [info, embeddings],
        scratch=[pltpu.VMEM((count, wide), BF16)],
    )[0]


def label_row(tail, first):
    turned = jnp.transpose(tail.astype(F32))
    label = turned[first : first + 1, :] * DIGIT + turned[first + 1 : first + 2, :]
    return jnp.where(turned[0:1, :] > 0, label, -1.0).astype(jnp.int32)


def label_col(tail, first):
    tail = tail.astype(F32)
    label = tail[:, first : first + 1] * DIGIT + tail[:, first + 1 : first + 2]
    return jnp.where(tail[:, 0:1] > 0, label, -1.0).astype(jnp.int32)


def sums_of(rows, label, children):
    count = rows.shape[0]
    member = one_hot(iota((children, count), 0) == label)
    sums = matmul(member, rows, ((1,), (0,)))
    return sums, matmul(jnp.ones((EXTRA, count), BF16), member, ((1,), (1,)))


def rows_of(arrived_ref):
    devices, slots, wide = arrived_ref.shape
    rows = arrived_ref[...].reshape(devices * slots, wide)
    return rows[:, : wide - LANES], rows[:, wide - LANES :]


def first_body(core_ref, arrived_ref, keep_ref, send_ref):
    rows, tail = rows_of(arrived_ref)
    width = rows.shape[1]
    parts, tall, _ = keep_ref.shape
    each = (tall - EXTRA) // (width // LANES)
    children = 2 * parts * each
    sums, counts = sums_of(rows, label_row(tail, 1), children)
    even = core_ref[0] == 0
    for j in range(width // LANES):
        at = slice(j * each, (j + 1) * each)
        piece = sums[:, j * LANES : (j + 1) * LANES].reshape(parts, 2, each, LANES)
        for y in range(parts):
            zero, one = piece[y, 0], piece[parts - 1 - y, 1]
            keep_ref[y, at, :] = jnp.where(even, zero, one).astype(BF16)
            send_ref[y, at, :] = jnp.where(even, one, zero).astype(BF16)
    for y in range(parts):
        blocks = (2 * y, 2 * (parts - 1 - y) + 1)
        chunks = [block * each // LANES * LANES for block in blocks]
        zero, one = [counts[:, chunk : chunk + LANES] for chunk in chunks]
        keep_ref[y, tall - EXTRA :, :] = jnp.where(even, zero, one).astype(BF16)
        send_ref[y, tall - EXTRA :, :] = jnp.where(even, one, zero).astype(BF16)


def first_sums(core, arrived, children, parts):
    devices, slots, wide = arrived.shape
    width = wide - LANES
    total = devices * slots
    half = (parts // 2, children // parts * (width // LANES) + EXTRA, LANES)
    return kernel_call(
        first_body,
        "first_sums",
        2 * total * children * width,
        [shaped(half), shaped(half)],
        [core, arrived],
        scalars=1,
    )


def residual_of(rows, tail, centers_ref):
    children = centers_ref.shape[0]
    picked = one_hot(iota((rows.shape[0], children), 1) == label_col(tail, 1))
    center = matmul(picked, centers_ref[...], ((1,), (0,)))
    return (rows.astype(F32) - center).astype(BF16)


def write_margins(rows, label, cents_ref, squares_ref, out_ref):
    scores = squares_ref[...] - 2.0 * matmul(rows, cents_ref[...], ((1,), (1,)))
    member = iota(scores.shape, 1) == label
    assigned = jnp.sum(jnp.where(member, scores, 0.0), axis=1, keepdims=True)
    margin = assigned - jnp.min(scores, axis=1, keepdims=True)
    costs = jnp.sum(jnp.where(member, margin, 0.0), axis=0, keepdims=True)
    high = costs.astype(BF16).astype(F32)
    chunks = costs.shape[1] // LANES
    index = iota(out_ref.shape, 0)
    out = jnp.zeros(out_ref.shape, F32)
    for q in range(chunks):
        lanes = slice(q * LANES, (q + 1) * LANES)
        out = jnp.where(index == q, high[:, lanes], out)
        out = jnp.where(index == q + chunks, (costs - high)[:, lanes], out)
    out_ref[...] = out.astype(BF16)


def margins_one_body(arrived_ref, cents_ref, squares_ref, out_ref, rows_ref):
    rows, tail = rows_of(arrived_ref)
    rows_ref[:, : rows.shape[1]] = rows
    rows_ref[:, rows.shape[1] :] = tail
    write_margins(rows, label_col(tail, 1), cents_ref, squares_ref, out_ref)


def margins_two_body(rows_ref, centers_ref, cents_ref, squares_ref, out_ref):
    width = cents_ref.shape[1]
    rows, tail = rows_ref[:, :width], rows_ref[:, width:]
    residual = residual_of(rows, tail, centers_ref)
    write_margins(residual, label_col(tail, 3), cents_ref, squares_ref, out_ref)


def margins_one(arrived, centroids, squares):
    devices, slots, wide = arrived.shape
    return kernel_call(
        margins_one_body,
        "margins_one",
        2 * devices * slots * centroids.size,
        [shaped((EXTRA, LANES)), shaped((devices * slots, wide))],
        [arrived, centroids, squares],
    )


def margins_two(rows, centers, centroids, squares):
    return kernel_call(
        margins_two_body,
        "margins_two",
        4 * rows.shape[0] * centroids.size,
        [shaped((EXTRA, LANES))],
        [rows, centers, centroids, squares],
    )[0]


def merge_body(mine_ref, arrived_ref, old_ref, costs_ref, out_ref):
    copies, tall, _ = out_ref.shape
    width = old_ref.shape[1]
    each = (tall - EXTRA) // (width // LANES)
    total = jnp.sum(arrived_ref[...].astype(F32), axis=0)
    counts = total[tall - EXTRA : tall - EXTRA + 1, :]
    first = mine_ref[0] * each
    mask = iota((each, LANES), 1) == iota((each, LANES), 0) + lax.rem(first, LANES)
    count = jnp.sum(jnp.where(mask, counts, 0.0), axis=1, keepdims=True)
    old_all = old_ref[pl.ds(pl.multiple_of(first, each), each), :].astype(F32)
    for j in range(width // LANES):
        old = old_all[:, j * LANES : (j + 1) * LANES]
        fresh = (total[j * each : (j + 1) * each, :] + old) / (count + 1.0)
        out_ref[:, j * each : (j + 1) * each, :] = jnp.broadcast_to(
            fresh.astype(BF16)[None], (copies, each, LANES)
        )
    out_ref[:, tall - EXTRA :, :] = jnp.broadcast_to(costs_ref[...][None], (copies, EXTRA, LANES))


def merge(mine, arrived, centroids, costs, copies):
    return kernel_call(
        merge_body,
        "merge",
        arrived.size,
        [shaped((copies,) + arrived.shape[1:])],
        [mine, arrived, centroids, costs],
        scalars=1,
    )[0]


def cost_sum(costs, chunks):
    total = jnp.sum(costs.astype(F32), axis=0)
    return total[0:chunks, :] + total[chunks : 2 * chunks, :]


def second_body(core_ref, rows_ref, own_ref, other_ref, new_ref, cost_ref, out_ref):
    parts, tall, _ = own_ref.shape
    children, width = new_ref.shape
    each = children // (2 * parts)
    core = core_ref[0]
    for ref, side in ((own_ref, core), (other_ref, 1 - core)):
        for y in range(parts):
            block = 2 * mirror(y, parts, side) + side
            at = pl.ds(pl.multiple_of(block * each, each), each)
            for j in range(width // LANES):
                new_ref[at, j * LANES : (j + 1) * LANES] = ref[y, j * each : (j + 1) * each, :]
    chunks = children // LANES
    cost_ref[...] = cost_sum(own_ref[:, tall - EXTRA :, :], chunks) + cost_sum(
        other_ref[:, tall - EXTRA :, :], chunks
    )
    rows, tail = rows_ref[:, :width], rows_ref[:, width:]
    sums, counts = sums_of(residual_of(rows, tail, new_ref), label_row(tail, 3), children)
    nx, nz, tall, _ = out_ref.shape
    each = children // (nx * nz)
    for j in range(width // LANES):
        piece = sums[:, j * LANES : (j + 1) * LANES].astype(BF16).reshape(nz, nx, each, LANES)
        for x in range(nx):
            out_ref[x, :, j * each : (j + 1) * each, :] = piece[:, x]
    for z in range(nz):
        for x in range(nx):
            chunk = (z * nx + x) * each // LANES * LANES
            out_ref[x, z, tall - EXTRA :, :] = counts[:, chunk : chunk + LANES].astype(BF16)


def second_sums(core, rows, own, other, children, nx, nz):
    total, wide = rows.shape
    width = wide - LANES
    tall = children // (nx * nz) * (width // LANES) + EXTRA
    return kernel_call(
        second_body,
        "second_sums",
        4 * total * children * width,
        [
            shaped((children, width)),
            shaped((children // LANES, LANES), F32),
            shaped((nx, nz, tall, LANES)),
        ],
        [core, rows, own, other],
        scalars=1,
    )


def last_body(full_ref, new_ref, cost_ref):
    nx, nz, tall, _ = full_ref.shape
    children, width = new_ref.shape
    each = children // (nx * nz)
    for x in range(nx):
        for z in range(nz):
            at = slice((z * nx + x) * each, (z * nx + x + 1) * each)
            for j in range(width // LANES):
                lanes = slice(j * LANES, (j + 1) * LANES)
                new_ref[at, lanes] = full_ref[x, z, j * each : (j + 1) * each, :]
    chunks = children // LANES
    cost_ref[...] = sum(cost_sum(full_ref[x, :, tall - EXTRA :, :], chunks) for x in range(nx))


def last(full, children, width):
    return kernel_call(
        last_body,
        "last",
        full.size,
        [shaped((children, width)), shaped((children // LANES, LANES), F32)],
        [full],
    )


def squares_of(centroids):
    cent_f = centroids.astype(F32)
    return jnp.sum(cent_f * cent_f, axis=1)[None, :]


def local(embeddings, cluster_key, child_first, child_second, coarse_centroids, fine_centroids):
    n_shard = lax.axis_size(SHARD)
    n_group = lax.axis_size(GROUP)
    rows_dev = embeddings.shape[0]
    children = coarse_centroids.shape[1]
    width = embeddings.shape[1]
    devices = n_shard * n_group
    coarse, fine = coarse_centroids[0], fine_centroids[0]
    core = lax.axis_index("core").astype(jnp.int32)[None]
    group = lax.axis_index(GROUP).astype(jnp.int32)[None]
    shard = lax.axis_index(SHARD).astype(jnp.int32)[None]

    info = jnp.stack(
        [cluster_key[:, 0], child_first, child_second] + [jnp.zeros((rows_dev,), jnp.int32)] * 5
    )
    layout = place(info, embeddings, devices)
    layout, core, group, shard = lax.optimization_barrier((layout, core, group, shard))
    arrived = exchange(layout, ALL)

    keep, send = first_sums(core, arrived, children, n_group)
    taken = lax.ppermute(send, "core", SWAP)
    parts_one = mirrored((keep.astype(F32) + taken.astype(F32)).astype(BF16))
    costs_one, rows = margins_one(arrived, coarse, squares_of(coarse))
    copies_one = merge(group, parts_one, coarse, costs_one, lax.axis_size("y"))
    own = mirrored(copies_one)
    other = lax.ppermute(own, "core", SWAP)

    nx, nz = lax.axis_size("x"), lax.axis_size("z")
    coarse_new, coarse_cost, partial_two = second_sums(core, rows, own, other, children, nx, nz)
    parts_two = jnp.sum(exchange(partial_two, "x").astype(F32), axis=0).astype(BF16)
    parts_two = exchange(parts_two, "z")
    costs_two = margins_two(rows, coarse_new, fine, squares_of(fine))
    copies_two = exchange(merge(shard, parts_two, fine, costs_two, nz), "z")
    full_two = jnp.broadcast_to(copies_two[None], (nx,) + copies_two.shape)
    fine_new, fine_cost = last(exchange(full_two, "x"), children, width)
    return (
        coarse_new[None],
        fine_new[None],
        coarse_cost.reshape(1, children),
        fine_cost.reshape(1, children),
    )


def solution(mesh):
    torus = Mesh(mesh.devices.reshape(-1, 4, mesh.shape["group"] // 2, 2), ALL)
    placed = (
        P(ALL, None),
        P(ALL, None),
        P(ALL),
        P(ALL),
        P(SHARD, None, None),
        P(GROUP, None, None),
    )
    return jax.shard_map(
        local,
        mesh=torus,
        in_specs=placed,
        out_specs=(
            P(SHARD, None, None),
            P(GROUP, None, None),
            P(SHARD, None),
            P(GROUP, None),
        ),
        check_vma=False,
    )
```

```python
import jax
import jax.numpy as jnp
from jax import lax
from jax.experimental import pallas as pl
from jax.experimental.pallas import tpu as pltpu
from jax.sharding import Mesh
from jax.sharding import PartitionSpec as P

SHARD = ("z", "x")
GROUP = ("y", "core")
ALL = SHARD + GROUP
SWAP = [(0, 1), (1, 0)]
SLOTS = 2
LANES = 128
EXTRA = 8
PIECES = 2
VMEM_BYTES = 32 * 2**20
DIGIT = 16
F32 = jnp.float32
BF16 = jnp.bfloat16


def exchange(blocks, axes):
    return lax.all_to_all(blocks, axes, split_axis=0, concat_axis=0, tiled=True)


def mirrored(blocks):
    n = lax.axis_size("y")
    groups = [[2 * i for i in range(n)], [2 * (n - 1 - i) + 1 for i in range(n)]]
    return lax.all_to_all(
        blocks, GROUP, split_axis=0, concat_axis=0, tiled=True, axis_index_groups=groups
    )


def mirror(index, count, core):
    return index + core * (count - 1 - 2 * index)


def iota(shape, dim):
    return lax.broadcasted_iota(jnp.int32, shape, dim)


def matmul(a, b, dims):
    return lax.dot_general(a, b, (dims, ((), ())), preferred_element_type=F32)


def kernel_call(body, name, flops, outs, args, scalars=0, scratch=()):
    moved = sum(x.size * x.dtype.itemsize for x in list(outs) + list(args))
    specs = [pl.BlockSpec(memory_space=pltpu.SMEM)] * scalars
    specs += [pl.BlockSpec(memory_space=pltpu.VMEM)] * (len(args) - scalars)
    return pl.pallas_call(
        body,
        name=name,
        in_specs=specs,
        out_specs=[pl.BlockSpec(memory_space=pltpu.VMEM)] * len(outs),
        out_shape=list(outs),
        scratch_shapes=list(scratch),
        cost_estimate=pl.CostEstimate(flops=flops, bytes_accessed=moved, transcendentals=0),
        compiler_params=pltpu.CompilerParams(vmem_limit_bytes=VMEM_BYTES),
    )(*args)


def shaped(shape, dtype=BF16):
    return jax.ShapeDtypeStruct(shape, dtype)


def one_hot(mask):
    return mask.astype(F32).astype(BF16)


def place_body(info_ref, emb_ref, out_ref, wide_ref):
    count, width = emb_ref.shape
    devices, slots, wide = out_ref.shape
    info = info_ref[...]
    turned = jnp.transpose(info.astype(F32)).astype(jnp.int32)
    keys_row, keys_col = info[0:1, :], turned[:, 0:1]
    earlier = (keys_col == keys_row) & (iota((count, count), 0) < iota((count, count), 1))
    rank = jnp.sum(earlier.astype(jnp.int32), axis=0, keepdims=True)
    target = keys_row * slots + rank
    one, two = turned[:, 1:2], turned[:, 2:3]
    lane = iota((count, LANES), 1)
    codes = jnp.where(lane == 0, 1, 0)
    for index, value in enumerate((one // DIGIT, one % DIGIT, two // DIGIT, two % DIGIT)):
        codes = jnp.where(lane == index + 1, value, codes)
    wide_ref[:, :width] = emb_ref[...]
    wide_ref[:, width:] = codes.astype(F32).astype(BF16)
    block = devices // PIECES
    for piece in range(PIECES):
        at = iota((block * slots, count), 0) + piece * block * slots
        moved = matmul(one_hot(at == target), wide_ref[...], ((1,), (0,))).astype(BF16)
        out_ref[piece * block : (piece + 1) * block] = moved.reshape(block, slots, wide)


def place(info, embeddings, devices):
    count, width = embeddings.shape
    wide = width + LANES
    return kernel_call(
        place_body,
        "place",
        2 * devices * SLOTS * count * wide,
        [shaped((devices, SLOTS, wide))],
        [info, embeddings],
        scratch=[pltpu.VMEM((count, wide), BF16)],
    )[0]


def label_row(tail, first):
    turned = jnp.transpose(tail.astype(F32))
    label = turned[first : first + 1, :] * DIGIT + turned[first + 1 : first + 2, :]
    return jnp.where(turned[0:1, :] > 0, label, -1.0).astype(jnp.int32)


def label_col(tail, first):
    tail = tail.astype(F32)
    label = tail[:, first : first + 1] * DIGIT + tail[:, first + 1 : first + 2]
    return jnp.where(tail[:, 0:1] > 0, label, -1.0).astype(jnp.int32)


def sums_of(rows, label, children):
    count = rows.shape[0]
    member = one_hot(iota((children, count), 0) == label)
    sums = matmul(member, rows, ((1,), (0,)))
    return sums, matmul(jnp.ones((EXTRA, count), BF16), member, ((1,), (1,)))


def rows_of(arrived_ref):
    devices, slots, wide = arrived_ref.shape
    rows = arrived_ref[...].reshape(devices * slots, wide)
    return rows[:, : wide - LANES], rows[:, wide - LANES :]


def first_body(core_ref, arrived_ref, keep_ref, send_ref):
    rows, tail = rows_of(arrived_ref)
    width = rows.shape[1]
    parts, tall, _ = keep_ref.shape
    each = (tall - EXTRA) // (width // LANES)
    children = 2 * parts * each
    sums, counts = sums_of(rows, label_row(tail, 1), children)
    even = core_ref[0] == 0
    for j in range(width // LANES):
        at = slice(j * each, (j + 1) * each)
        piece = sums[:, j * LANES : (j + 1) * LANES].reshape(parts, 2, each, LANES)
        for y in range(parts):
            zero, one = piece[y, 0], piece[parts - 1 - y, 1]
            keep_ref[y, at, :] = jnp.where(even, zero, one).astype(BF16)
            send_ref[y, at, :] = jnp.where(even, one, zero).astype(BF16)
    for y in range(parts):
        blocks = (2 * y, 2 * (parts - 1 - y) + 1)
        chunks = [block * each // LANES * LANES for block in blocks]
        zero, one = [counts[:, chunk : chunk + LANES] for chunk in chunks]
        keep_ref[y, tall - EXTRA :, :] = jnp.where(even, zero, one).astype(BF16)
        send_ref[y, tall - EXTRA :, :] = jnp.where(even, one, zero).astype(BF16)


def first_sums(core, arrived, children, parts):
    devices, slots, wide = arrived.shape
    width = wide - LANES
    total = devices * slots
    half = (parts // 2, children // parts * (width // LANES) + EXTRA, LANES)
    return kernel_call(
        first_body,
        "first_sums",
        2 * total * children * width,
        [shaped(half), shaped(half)],
        [core, arrived],
        scalars=1,
    )


def residual_of(rows, tail, centers_ref):
    children = centers_ref.shape[0]
    picked = one_hot(iota((rows.shape[0], children), 1) == label_col(tail, 1))
    center = matmul(picked, centers_ref[...], ((1,), (0,)))
    return (rows.astype(F32) - center).astype(BF16)


def write_margins(rows, label, cents_ref, squares_ref, out_ref):
    scores = squares_ref[...] - 2.0 * matmul(rows, cents_ref[...], ((1,), (1,)))
    member = iota(scores.shape, 1) == label
    assigned = jnp.sum(jnp.where(member, scores, 0.0), axis=1, keepdims=True)
    margin = assigned - jnp.min(scores, axis=1, keepdims=True)
    costs = jnp.sum(jnp.where(member, margin, 0.0), axis=0, keepdims=True)
    high = costs.astype(BF16).astype(F32)
    chunks = costs.shape[1] // LANES
    index = iota(out_ref.shape, 0)
    out = jnp.zeros(out_ref.shape, F32)
    for q in range(chunks):
        lanes = slice(q * LANES, (q + 1) * LANES)
        out = jnp.where(index == q, high[:, lanes], out)
        out = jnp.where(index == q + chunks, (costs - high)[:, lanes], out)
    out_ref[...] = out.astype(BF16)


def margins_one_body(arrived_ref, cents_ref, squares_ref, out_ref, rows_ref):
    rows, tail = rows_of(arrived_ref)
    rows_ref[:, : rows.shape[1]] = rows
    rows_ref[:, rows.shape[1] :] = tail
    write_margins(rows, label_col(tail, 1), cents_ref, squares_ref, out_ref)


def margins_two_body(rows_ref, centers_ref, cents_ref, squares_ref, out_ref):
    width = cents_ref.shape[1]
    rows, tail = rows_ref[:, :width], rows_ref[:, width:]
    residual = residual_of(rows, tail, centers_ref)
    write_margins(residual, label_col(tail, 3), cents_ref, squares_ref, out_ref)


def margins_one(arrived, centroids, squares):
    devices, slots, wide = arrived.shape
    return kernel_call(
        margins_one_body,
        "margins_one",
        2 * devices * slots * centroids.size,
        [shaped((EXTRA, LANES)), shaped((devices * slots, wide))],
        [arrived, centroids, squares],
    )


def margins_two(rows, centers, centroids, squares):
    return kernel_call(
        margins_two_body,
        "margins_two",
        4 * rows.shape[0] * centroids.size,
        [shaped((EXTRA, LANES))],
        [rows, centers, centroids, squares],
    )[0]


def merge_body(mine_ref, arrived_ref, old_ref, costs_ref, out_ref):
    copies, tall, _ = out_ref.shape
    width = old_ref.shape[1]
    each = (tall - EXTRA) // (width // LANES)
    total = jnp.sum(arrived_ref[...].astype(F32), axis=0)
    counts = total[tall - EXTRA : tall - EXTRA + 1, :]
    first = mine_ref[0] * each
    mask = iota((each, LANES), 1) == iota((each, LANES), 0) + lax.rem(first, LANES)
    count = jnp.sum(jnp.where(mask, counts, 0.0), axis=1, keepdims=True)
    old_all = old_ref[pl.ds(pl.multiple_of(first, each), each), :].astype(F32)
    for j in range(width // LANES):
        old = old_all[:, j * LANES : (j + 1) * LANES]
        fresh = (total[j * each : (j + 1) * each, :] + old) / (count + 1.0)
        out_ref[:, j * each : (j + 1) * each, :] = jnp.broadcast_to(
            fresh.astype(BF16)[None], (copies, each, LANES)
        )
    out_ref[:, tall - EXTRA :, :] = jnp.broadcast_to(costs_ref[...][None], (copies, EXTRA, LANES))


def merge(mine, arrived, centroids, costs, copies):
    return kernel_call(
        merge_body,
        "merge",
        arrived.size,
        [shaped((copies,) + arrived.shape[1:])],
        [mine, arrived, centroids, costs],
        scalars=1,
    )[0]


def cost_sum(costs, chunks):
    total = jnp.sum(costs.astype(F32), axis=0)
    return total[0:chunks, :] + total[chunks : 2 * chunks, :]


def second_body(core_ref, rows_ref, own_ref, other_ref, new_ref, cost_ref, out_ref):
    parts, tall, _ = own_ref.shape
    children, width = new_ref.shape
    each = children // (2 * parts)
    core = core_ref[0]
    for ref, side in ((own_ref, core), (other_ref, 1 - core)):
        for y in range(parts):
            block = 2 * mirror(y, parts, side) + side
            at = pl.ds(pl.multiple_of(block * each, each), each)
            for j in range(width // LANES):
                new_ref[at, j * LANES : (j + 1) * LANES] = ref[y, j * each : (j + 1) * each, :]
    chunks = children // LANES
    cost_ref[...] = cost_sum(own_ref[:, tall - EXTRA :, :], chunks) + cost_sum(
        other_ref[:, tall - EXTRA :, :], chunks
    )
    rows, tail = rows_ref[:, :width], rows_ref[:, width:]
    sums, counts = sums_of(residual_of(rows, tail, new_ref), label_row(tail, 3), children)
    nx, nz, tall, _ = out_ref.shape
    each = children // (nx * nz)
    for j in range(width // LANES):
        piece = sums[:, j * LANES : (j + 1) * LANES].astype(BF16).reshape(nz, nx, each, LANES)
        for x in range(nx):
            out_ref[x, :, j * each : (j + 1) * each, :] = piece[:, x]
    for z in range(nz):
        for x in range(nx):
            chunk = (z * nx + x) * each // LANES * LANES
            out_ref[x, z, tall - EXTRA :, :] = counts[:, chunk : chunk + LANES].astype(BF16)


def second_sums(core, rows, own, other, children, nx, nz):
    total, wide = rows.shape
    width = wide - LANES
    tall = children // (nx * nz) * (width // LANES) + EXTRA
    return kernel_call(
        second_body,
        "second_sums",
        4 * total * children * width,
        [
            shaped((children, width)),
            shaped((children // LANES, LANES), F32),
            shaped((nx, nz, tall, LANES)),
        ],
        [core, rows, own, other],
        scalars=1,
    )


def last_body(full_ref, new_ref, cost_ref):
    nx, nz, tall, _ = full_ref.shape
    children, width = new_ref.shape
    each = children // (nx * nz)
    for x in range(nx):
        for z in range(nz):
            at = slice((z * nx + x) * each, (z * nx + x + 1) * each)
            for j in range(width // LANES):
                lanes = slice(j * LANES, (j + 1) * LANES)
                new_ref[at, lanes] = full_ref[x, z, j * each : (j + 1) * each, :]
    chunks = children // LANES
    cost_ref[...] = sum(cost_sum(full_ref[x, :, tall - EXTRA :, :], chunks) for x in range(nx))


def last(full, children, width):
    return kernel_call(
        last_body,
        "last",
        full.size,
        [shaped((children, width)), shaped((children // LANES, LANES), F32)],
        [full],
    )


def squares_of(centroids):
    cent_f = centroids.astype(F32)
    return jnp.sum(cent_f * cent_f, axis=1)[None, :]


def local(embeddings, cluster_key, child_first, child_second, coarse_centroids, fine_centroids):
    n_shard = lax.axis_size(SHARD)
    n_group = lax.axis_size(GROUP)
    rows_dev = embeddings.shape[0]
    children = coarse_centroids.shape[1]
    width = embeddings.shape[1]
    devices = n_shard * n_group
    coarse, fine = coarse_centroids[0], fine_centroids[0]
    core = lax.axis_index("core").astype(jnp.int32)[None]
    group = lax.axis_index(GROUP).astype(jnp.int32)[None]
    shard = lax.axis_index(SHARD).astype(jnp.int32)[None]

    info = jnp.stack(
        [cluster_key[:, 0], child_first, child_second] + [jnp.zeros((rows_dev,), jnp.int32)] * 5
    )
    layout = place(info, embeddings, devices)
    layout, core, group, shard = lax.optimization_barrier((layout, core, group, shard))
    arrived = exchange(layout, ALL)

    keep, send = first_sums(core, arrived, children, n_group)
    taken = lax.ppermute(send, "core", SWAP)
    parts_one = mirrored((keep.astype(F32) + taken.astype(F32)).astype(BF16))
    costs_one, rows = margins_one(arrived, coarse, squares_of(coarse))
    copies_one = merge(group, parts_one, coarse, costs_one, lax.axis_size("y"))
    own = mirrored(copies_one)
    other = lax.ppermute(own, "core", SWAP)

    nx, nz = lax.axis_size("x"), lax.axis_size("z")
    coarse_new, coarse_cost, partial_two = second_sums(core, rows, own, other, children, nx, nz)
    parts_two = exchange(partial_two.reshape((n_shard,) + partial_two.shape[2:]), ("x", "z"))
    costs_two = margins_two(rows, coarse_new, fine, squares_of(fine))
    copies_two = exchange(merge(shard, parts_two, fine, costs_two, nz), "z")
    full_two = jnp.broadcast_to(copies_two[None], (nx,) + copies_two.shape)
    fine_new, fine_cost = last(exchange(full_two, "x"), children, width)
    return (
        coarse_new[None],
        fine_new[None],
        coarse_cost.reshape(1, children),
        fine_cost.reshape(1, children),
    )


def solution(mesh):
    torus = Mesh(mesh.devices.reshape(-1, 4, mesh.shape["group"] // 2, 2), ALL)
    placed = (
        P(ALL, None),
        P(ALL, None),
        P(ALL),
        P(ALL),
        P(SHARD, None, None),
        P(GROUP, None, None),
    )
    return jax.shard_map(
        local,
        mesh=torus,
        in_specs=placed,
        out_specs=(
            P(SHARD, None, None),
            P(GROUP, None, None),
            P(SHARD, None),
            P(GROUP, None),
        ),
        check_vma=False,
    )
```
